32 devices in a mesh: ctx: 2 (over x), clu: 4 (over z), tp: 4 (over y, core).
Axes of the slice: x: 2, y: 2, z: 4, core: 2. Of those that a mesh axis runs over, the one named last changes fastest.
Arguments:
- tokens: bfloat16 [2, 1024, 4096], P('ctx', 'clu'), may hold values from -32 to 32
- proj_weight: bfloat16 [4096, 2, 2048], P(('ctx', 'clu'), None, 'tp'), may hold values from -0.09375 to 0.09375
- clusters: int32 [2, 1024, 16], P('ctx', 'clu', 'tp'), may hold values from 0 to 63, as said below
Outputs:
- attended: bfloat16 [2, 1024, 2048], P('ctx', 'clu', 'tp')
The draws below stay inside these ranges and needn't reach their ends.
Inputs may be any that keep to these rules, and one draw needn't show every extreme that they name: `clusters`: owner k of head h holds ids k * 16 to (k + 1) * 16 - 1. In each aligned block of 256 positions of a sequence, for every head, at most 128 positions have ids of one owner; for each sequence and head one owner has exactly 128 positions in every block.
All inputs are finite; a program needn't handle non-finite values.
Results may differ from the reference program's by a relative error of at most 0.0068.
Values may be sent and summed in bfloat16 or wider, within the bound.
A program may use at most 64 MiB of HBM per device.

```python
import jax
import jax.numpy as jnp
from jax import lax

D = 4096
HEADS = 16
DH = 128
CLUSTERS = 64
TOK_DEV = 256
SEQ_LEN = 1024
SEQS = 2
CAP = 128


def draw_clusters(key, part):
    key = jax.random.fold_in(key, 11)
    owners = SEQ_LEN // TOK_DEV
    per_owner = CLUSTERS // owners
    slots_all = owners * CAP
    hot_key, score_key, perm_key, pick_key = jax.random.split(key, 4)
    hot_owner = jax.random.randint(hot_key, (SEQS, HEADS), 0, owners)
    scores = jax.random.randint(score_key, (SEQS, owners, HEADS, slots_all), 0, 65536)
    slot_ids = jnp.arange(slots_all, dtype=jnp.int32)
    slot_owner = slot_ids // CAP
    ranked = scores * slots_all + slot_ids[None, None, None, :]
    is_hot = slot_owner[None, None, None, :] == hot_owner[:, None, :, None]
    ranked = jnp.where(is_hot, slot_ids[None, None, None, :] - slots_all, ranked)
    ordering = jnp.argsort(ranked, axis=-1)[..., :TOK_DEV]
    chosen = (ordering // CAP).astype(jnp.int32)
    chosen = jax.random.permutation(perm_key, chosen, axis=-1, independent=True)
    within = jax.random.randint(pick_key, chosen.shape, 0, per_owner)
    cluster_ids = chosen * per_owner + within
    return cluster_ids.transpose(0, 1, 3, 2).reshape(SEQS, SEQ_LEN, HEADS).astype(jnp.int32)


def draw_tokens(key, part):
    key = jax.random.fold_in(key, 5)
    noise_key = jax.random.fold_in(key, 0)
    values = jnp.clip(jax.random.normal(noise_key, (SEQS, SEQ_LEN, D), jnp.float32), -6.0, 6.0)
    return values.astype(jnp.bfloat16)


def steps_of(key, dims, cuts, low, top_value):
    def one(axis_at, parts):
        heights = jax.random.uniform(jax.random.fold_in(jax.random.fold_in(key, 6), axis_at), (parts,), jnp.float32, low / len(cuts), top_value / len(cuts))
        return jnp.repeat(jnp.exp(heights), dims[axis_at] // parts).reshape((-1,) + (1,) * (len(dims) - axis_at - 1))

    gain = one(*cuts[0])
    for cut in cuts[1:]:
        gain = gain * one(*cut)
    return gain


def centred(stream_key, extent, spread, most, cuts=(), held_as=jnp.bfloat16):
    values = jax.random.normal(stream_key, extent, jnp.float32) * spread
    if len(cuts) > 0:
        values = steps_of(stream_key, extent, cuts, -0.22, 0.18) * values
    return jnp.clip(values, min=-most, max=most).astype(held_as)


def setup_inputs(seed: int = 0) -> dict:
    keys = jax.random.split(jax.random.key(seed), 4)
    tokens = draw_tokens(jax.random.fold_in(keys[3], 71), 0)
    proj_weight = centred(keys[1], (D, 2, HEADS * DH), D ** -0.5, 0.09375, ((0, 8), (2, 4)))
    clusters = draw_clusters(jax.random.fold_in(keys[3], 71), 0)
    return dict(tokens=tokens, proj_weight=proj_weight, clusters=clusters)


def reference(tokens, proj_weight, clusters):
    flattened = tokens.reshape(SEQS * SEQ_LEN, D)
    projected = jnp.dot(flattened, proj_weight.reshape(D, 2 * HEADS * DH), preferred_element_type=jnp.float32).astype(jnp.bfloat16)
    projected = projected.reshape(SEQS, SEQ_LEN, 2, HEADS, DH)
    key_rows = projected[:, :, 0].transpose(0, 2, 1, 3).reshape(SEQS * HEADS, SEQ_LEN, DH)
    value_rows = projected[:, :, 1].transpose(0, 2, 1, 3).reshape(SEQS * HEADS, SEQ_LEN, DH)
    cluster_ids = clusters.transpose(0, 2, 1).reshape(SEQS * HEADS, SEQ_LEN).astype(jnp.int32)
    block_rows = 1024 if SEQ_LEN % 1024 == 0 else SEQ_LEN
    score_scale = DH ** -0.5
    key_pos = jnp.arange(SEQ_LEN, dtype=jnp.int32)

    def one_head(inputs):
        head_keys, head_values, head_ids = inputs

        def query_block(first_row):
            first_row = first_row.astype(jnp.int32)
            query_rows = lax.dynamic_slice_in_dim(head_keys, first_row, block_rows, 0)
            query_ids = lax.dynamic_slice_in_dim(head_ids, first_row, block_rows, 0)
            query_pos = first_row + jnp.arange(block_rows, dtype=jnp.int32)
            scores = jnp.dot(query_rows, head_keys.T, preferred_element_type=jnp.float32) * score_scale
            admitted = (query_ids[:, None] == head_ids[None, :]) & (key_pos[None, :] <= query_pos[:, None])
            scores = jnp.where(key_pos[None, :] == query_pos[:, None], -100000.0, scores)
            scores = jnp.where(admitted, scores, -1e30)
            row_max = jnp.max(scores, axis=1, keepdims=True)
            exp_scores = jnp.exp(scores - row_max)
            row_total = jnp.sum(exp_scores, axis=1, keepdims=True)
            probabilities = (exp_scores / row_total).astype(jnp.bfloat16)
            return jnp.dot(probabilities, head_values, preferred_element_type=jnp.float32).astype(jnp.bfloat16)

        starts = jnp.arange(SEQ_LEN // block_rows, dtype=jnp.int32) * block_rows
        return lax.map(query_block, starts).reshape(SEQ_LEN, DH)

    attended = lax.map(one_head, (key_rows, value_rows, cluster_ids))
    attended = attended.reshape(SEQS, HEADS, SEQ_LEN, DH).transpose(0, 2, 1, 3)
    return attended.reshape(SEQS, SEQ_LEN, HEADS * DH)
```

```python
import functools

import jax
import jax.numpy as jnp
from jax import lax
from jax.experimental import pallas as pl
from jax.experimental.pallas import tpu as pltpu
from jax.sharding import PartitionSpec as P

CLUSTERS = 64
MESH = pl.DeviceIdType.MESH


def head_kernel(
    owners, depth, head_dim, score_scale,
    tok_ref, w_ref, cl_ref, out_ref,
    rows, weights, ids, proj, reply,
    own_sem, wz_send, wz_recv, wx_send, wx_recv, id_send, id_recv,
    hop_send, hop_recv, core_send, core_recv, y_send, y_recv, far_send, far_recv,
    out_send, out_recv,
):
    a = lax.axis_index("ctx")
    c = lax.axis_index("clu")
    t = lax.axis_index("tp")
    k = lax.rem(t, 2)
    y = t // 2
    count = tok_ref.shape[0]
    quarter = tok_ref.shape[1] // 4
    last = owners - 1
    core_peer = {"tp": y * 2 + 1 - k}
    y_peer = {"tp": (1 - y) * 2 + k}
    x_peer = {"ctx": 1 - a}

    def at_clu(index):
        return {"clu": index}

    def remote(src, dst, send, recv, peer):
        return pltpu.make_async_remote_copy(
            src_ref=src, dst_ref=dst, send_sem=send, recv_sem=recv,
            device_id=peer, device_id_type=MESH,
        )

    def features(q):
        return pl.ds(pl.multiple_of(q * quarter, quarter), quarter)

    def piece(ctx, clu):
        return weights.at[pl.ds(pl.multiple_of((ctx * owners + clu) * depth, depth), depth)]

    barrier = pltpu.get_barrier_semaphore()
    others = [at_clu(lax.rem(c + d, owners)) for d in range(1, owners)]
    others += [core_peer, y_peer, x_peer]
    for peer in others:
        pl.semaphore_signal(barrier, inc=1, device_id=peer, device_id_type=MESH)
    own_rows = pltpu.make_async_copy(tok_ref, rows.at[c], own_sem.at[0])
    own_piece = pltpu.make_async_copy(w_ref.at[c], piece(a, c), own_sem.at[1])
    own_ids = pltpu.make_async_copy(cl_ref.at[c], ids.at[c], own_sem.at[2])
    for copy in (own_rows, own_piece, own_ids):
        copy.start()
    pl.semaphore_wait(barrier, len(others))

    def hop(side, step):
        block = c - step if side == 0 else c + step
        src = rows.at[block, :, features(t)] if step else tok_ref.at[:, features(t)]
        return remote(
            src, rows.at[block, :, features(t)],
            hop_send.at[side, step], hop_recv.at[side, step],
            at_clu(c + 1 if side == 0 else c - 1),
        )

    def hop_sends(side, step):
        if side == 0:
            return (c >= step) & (c < last)
        return (c + step <= last) & (c > 0)

    def came(side, step):
        block = c - 1 - step if side == 0 else c + 1 + step
        return block, ((block >= 0) if side == 0 else (block <= last))

    def landed(block, q, send, recv, peer):
        here = rows.at[block, :, features(q)]
        return remote(here, here, send, recv, peer)

    def to_core(side, step, block, q):
        return landed(block, q, core_send.at[side, step], core_recv.at[side, step], core_peer)

    def to_y(side, step, block, q):
        return landed(block, q, y_send.at[side, step], y_recv.at[side, step], y_peer)

    def to_core_far(side, step, block, q):
        return landed(block, q, far_send.at[side, step], far_recv.at[side, step], core_peer)

    def w_hop(d):
        goal = lax.rem(c + d, owners)
        return remote(w_ref.at[goal], piece(a, c), wz_send.at[d - 1], wz_recv.at[d - 1], at_clu(goal))

    def w_came(d):
        source = lax.rem(c + owners - d, owners)
        here = piece(a, source)
        return remote(here, here, wz_send.at[d - 1], wz_recv.at[d - 1], at_clu(source))

    def w_cross(d, ctx):
        here = piece(ctx, lax.rem(c + owners - d, owners))
        src = w_ref.at[c] if d == 0 else here
        return remote(src, here, wx_send.at[d], wx_recv.at[d], x_peer)

    def id_hop(d):
        goal = lax.rem(c + d, owners)
        return remote(cl_ref.at[goal], ids.at[c], id_send.at[d - 1], id_recv.at[d - 1], at_clu(goal))

    def id_came(d):
        source = lax.rem(c + owners - d, owners)
        return remote(ids.at[source], ids.at[source], id_send.at[d - 1], id_recv.at[d - 1], at_clu(source))

    for side in range(2):
        pl.when(hop_sends(side, 0))(lambda side=side: hop(side, 0).start())
    w_cross(0, a).start()
    for d in range(1, owners):
        w_hop(d).start()
    for d in range(1, owners):
        id_hop(d).start()

    def project(block):
        summed = jnp.dot(rows[block], weights[...], preferred_element_type=jnp.float32)
        proj[block] = summed.astype(jnp.bfloat16)

    def arrive(step):
        for side in range(2):
            block, here = came(side, step)

            @pl.when(here)
            def _(side=side, block=block):
                landed(block, t, hop_send.at[side, step], hop_recv.at[side, step], core_peer).wait_recv()
                to_y(side, step, block, t).start()
                to_core(side, step, block, t).start()

            if step + 1 < last:
                pl.when(hop_sends(side, step + 1))(lambda side=side: hop(side, step + 1).start())
        w_came(step + 1).wait_recv()
        w_cross(step + 1, a).start()

    def relay(step):
        for side in range(2):
            block, here = came(side, step)

            @pl.when(here)
            def _(side=side, block=block):
                to_y(side, step, block, (1 - y) * 2 + k).wait_recv()
                to_core_far(side, step, block, (1 - y) * 2 + k).start()

    def finish(step):
        for side in range(2):
            block, here = came(side, step)

            @pl.when(here)
            def _(side=side, block=block):
                to_core(side, step, block, y * 2 + 1 - k).wait_recv()
                to_core_far(side, step, block, (1 - y) * 2 + 1 - k).wait_recv()
                project(block)

    for step in range(last):
        arrive(step)
        if step > 0:
            relay(step - 1)
    for copy in (own_rows, own_piece, own_ids):
        copy.wait()
    for d in range(owners):
        w_cross(d, 1 - a).wait_recv()
    project(c)
    for step in range(last):
        if step == last - 1:
            relay(step)
        finish(step)
    for d in range(1, owners):
        id_came(d).wait_recv()

    def send_reply(goal):
        return remote(
            reply.at[goal], out_ref.at[:, pl.ds(pl.multiple_of(c * head_dim, head_dim), head_dim)],
            out_send.at[goal], out_recv.at[c], at_clu(goal),
        )

    def keep_reply(goal):
        return pltpu.make_async_copy(
            reply.at[goal], out_ref.at[:, pl.ds(pl.multiple_of(c * head_dim, head_dim), head_dim)],
            out_send.at[goal],
        )

    for goal in reversed(range(owners)):
        query = proj[goal, :, :head_dim]
        query_ids = jnp.transpose(ids[goal])[:, :1]
        parts = []
        for block in range(goal + 1):
            scores = lax.dot_general(
                query, proj[block, :, :head_dim], (((1,), (1,)), ((), ())),
                preferred_element_type=jnp.float32,
            ) * score_scale
            admitted = query_ids == ids[block, :1, :]
            if block == goal:
                at = lax.broadcasted_iota(jnp.int32, (count, count), 0)
                to = lax.broadcasted_iota(jnp.int32, (count, count), 1)
                scores = jnp.where(at == to, -100000.0, scores)
                admitted = admitted & (to <= at)
            parts.append(jnp.where(admitted, scores, -1e30))
        top = functools.reduce(jnp.maximum, [jnp.max(p, axis=1, keepdims=True) for p in parts])
        total = jnp.zeros((count, 1), jnp.float32)
        mixed = jnp.zeros((count, head_dim), jnp.float32)
        for block, part in enumerate(parts):
            part = jnp.exp(part - top)
            total += jnp.sum(part, axis=1, keepdims=True)
            mixed += jnp.dot(
                part.astype(jnp.bfloat16), proj[block, :, head_dim:],
                preferred_element_type=jnp.float32,
            )
        reply[goal] = (mixed / total).astype(jnp.bfloat16)
        pl.when(c != goal)(lambda goal=goal: send_reply(goal).start())
        pl.when(c == goal)(lambda goal=goal: keep_reply(goal).start())

    for step in range(last):
        for side in range(2):
            block, here = came(side, step)
            pl.when(hop_sends(side, step))(lambda side=side, step=step: hop(side, step).wait_send())

            @pl.when(here)
            def _(side=side, step=step, block=block):
                to_y(side, step, block, t).wait_send()
                to_core(side, step, block, t).wait_send()
                to_core_far(side, step, block, (1 - y) * 2 + k).wait_send()

    for d in range(1, owners):
        w_hop(d).wait_send()
        id_hop(d).wait_send()
    for d in range(owners):
        w_cross(d, a).wait_send()
    for goal in range(owners):
        @pl.when(c != goal)
        def _(goal=goal):
            send_reply(goal).wait_send()
            column = out_ref.at[:, pl.ds(goal * head_dim, head_dim)]
            remote(reply.at[goal], column, out_send.at[goal], out_recv.at[goal], at_clu(goal)).wait_recv()

        pl.when(c == goal)(lambda goal=goal: keep_reply(goal).wait())


def head_body(tokens, proj_weight, clusters):
    row_count, width = tokens.shape[1:]
    owners = lax.axis_size("clu")
    heads_here = clusters.shape[2]
    depth, _, proj_width = proj_weight.shape
    head_dim = proj_width // heads_here
    pieces = (
        proj_weight.reshape(depth, 2, heads_here, head_dim)
        .transpose(2, 0, 1, 3)
        .reshape(heads_here, depth, 2 * head_dim)
    )
    labels = jnp.broadcast_to(clusters[0].T[:, None, :], (heads_here, 8, row_count))
    steps = owners - 1
    dma = pltpu.SemaphoreType.DMA
    out = pl.pallas_call(
        functools.partial(head_kernel, owners, depth, head_dim, head_dim ** (-0.5)),
        out_shape=jax.ShapeDtypeStruct((row_count, proj_width), jnp.bfloat16),
        in_specs=[pl.BlockSpec(memory_space=pl.ANY)] * 3,
        out_specs=pl.BlockSpec(memory_space=pl.ANY),
        scratch_shapes=[
            pltpu.VMEM((owners, row_count, width), jnp.bfloat16),
            pltpu.VMEM((width, 2 * head_dim), jnp.bfloat16),
            pltpu.VMEM((owners, 8, row_count), jnp.int32),
            pltpu.VMEM((owners, row_count, 2 * head_dim), jnp.bfloat16),
            pltpu.VMEM((owners, row_count, head_dim), jnp.bfloat16),
            dma((3,)),
            dma((steps,)), dma((steps,)),
            dma((owners,)), dma((owners,)),
            dma((steps,)), dma((steps,)),
            dma((2, steps)), dma((2, steps)),
            dma((2, steps)), dma((2, steps)),
            dma((2, steps)), dma((2, steps)),
            dma((2, steps)), dma((2, steps)),
            dma((owners,)), dma((owners,)),
        ],
        compiler_params=pltpu.CompilerParams(
            collective_id=0, has_side_effects=True, vmem_limit_bytes=40 * 1024 * 1024
        ),
    )(tokens[0], pieces, labels)
    return out[None]


def body(tokens, proj_weight, clusters):
    local_rows = tokens[0]
    row_count = local_rows.shape[0]
    owners = lax.axis_size("clu")
    heads_here = clusters.shape[2]
    proj_width = proj_weight.shape[2]
    head_dim = proj_width // heads_here
    capacity = 2 * row_count // owners
    per_owner = CLUSTERS // owners
    length = row_count * owners
    total_slots = owners * capacity
    score_scale = head_dim ** (-0.5)
    weight_piece = lax.all_gather(proj_weight, ("ctx", "clu"), axis=0, tiled=True)
    flat_piece = weight_piece.reshape(weight_piece.shape[0], 2 * proj_width)
    summed = jnp.dot(local_rows, flat_piece, preferred_element_type=jnp.float32)
    projected = summed.astype(jnp.bfloat16)
    queries = projected[:, :proj_width].reshape(row_count, heads_here, head_dim)
    values = projected[:, proj_width:].reshape(row_count, heads_here, head_dim)
    features = jnp.concatenate([queries, values], axis=2).transpose(1, 0, 2)
    cluster_ids = clusters[0]
    owner_of = cluster_ids // per_owner
    onehot = (owner_of[:, :, None] == jnp.arange(owners, dtype=jnp.int32)[None, None, :]).astype(
        jnp.int32
    )
    rank_in = jnp.sum((jnp.cumsum(onehot, axis=0) - onehot) * onehot, axis=2)
    slot_of = (owner_of * capacity + rank_in).T
    head_rows = jnp.arange(heads_here, dtype=jnp.int32)[:, None]
    token_index = jnp.broadcast_to(
        jnp.arange(row_count, dtype=jnp.int32)[None, :], (heads_here, row_count)
    )
    source = jnp.zeros((heads_here, total_slots), jnp.int32).at[head_rows, slot_of].set(token_index)
    positions = lax.axis_index("clu") * row_count + jnp.arange(row_count, dtype=jnp.int32)
    labels = cluster_ids.T * length + positions[None, :]
    slot_tags = (
        jnp.full((heads_here, total_slots), -1, jnp.int32).at[head_rows, slot_of].set(labels)
    )
    outgoing = jnp.take_along_axis(features, source[:, :, None], axis=1)
    outgoing = jnp.where((slot_tags >= 0)[:, :, None], outgoing, jnp.zeros_like(outgoing))
    outgoing = outgoing.reshape(heads_here, owners, capacity, 2 * head_dim)
    slot_tags = slot_tags.reshape(heads_here, owners, capacity)

    def attend_head(head_item):
        slot_block, key_tags = head_item
        flattened = slot_block.reshape(-1, 2 * head_dim)
        key_rows = flattened[:, :head_dim]
        value_rows = flattened[:, head_dim:]
        key_tags = key_tags.reshape(-1)
        scores = (
            jnp.einsum("qd,kd->qk", key_rows, key_rows, preferred_element_type=jnp.float32)
            * score_scale
        )
        tag_group = key_tags // length
        tag_pos = key_tags % length
        admitted = (
            (key_tags[None, :] >= 0)
            & (tag_group[None, :] == tag_group[:, None])
            & (tag_pos[None, :] <= tag_pos[:, None])
        )
        scores = jnp.where(key_tags[None, :] == key_tags[:, None], -100000.0, scores)
        scores = jnp.where(admitted, scores, -1e30)
        row_max = jnp.max(scores, axis=1, keepdims=True)
        exp_scores = jnp.exp(scores - row_max)
        row_total = jnp.sum(exp_scores, axis=1, keepdims=True)
        probabilities = (exp_scores / row_total).astype(jnp.bfloat16)
        result = jnp.dot(probabilities, value_rows, preferred_element_type=jnp.float32).astype(
            jnp.bfloat16
        )
        return result.reshape(slot_block.shape[0], slot_block.shape[1], head_dim)

    replies = lax.map(
        attend_head,
        (
            lax.all_to_all(outgoing, "clu", split_axis=1, concat_axis=1, tiled=True),
            lax.all_to_all(slot_tags, "clu", split_axis=1, concat_axis=1, tiled=True),
        ),
    )
    returned = lax.all_to_all(replies, "clu", split_axis=1, concat_axis=1, tiled=True)
    returned = returned.reshape(heads_here, total_slots, head_dim)
    gathered = jnp.take_along_axis(returned, slot_of[:, :, None], axis=1)
    return gathered.transpose(1, 0, 2).reshape(1, row_count, heads_here * head_dim)


def solution(mesh):
    sizes = dict(mesh.shape)
    heads_here = 16 // sizes["tp"]
    by_head = sizes["ctx"] == 2 and sizes["tp"] == 4 and sizes["clu"] == heads_here
    return jax.shard_map(
        head_body if by_head else body,
        mesh=mesh,
        in_specs=(P("ctx", "clu", None), P(("ctx", "clu"), None, "tp"), P("ctx", "clu", "tp")),
        out_specs=P("ctx", "clu", "tp"),
        check_vma=False,
    )
```

```python
import functools

import jax
import jax.numpy as jnp
from jax import lax
from jax.experimental import pallas as pl
from jax.experimental.pallas import tpu as pltpu
from jax.sharding import PartitionSpec as P

CLUSTERS = 64
MESH = pl.DeviceIdType.MESH


def head_kernel(
    owners, depth, head_dim, score_scale,
    tok_ref, w_ref, cl_ref, out_ref,
    rows, weights, ids, mine, part, theirs, proj, reply,
    own_sem, wm_send, wm_recv, wx_send, wx_recv, id_send, id_recv,
    cross_send, cross_recv, fwd_send, fwd_recv, mate_send, mate_recv,
    core_send, core_recv, y_send, y_recv, far_send, far_recv,
    part_send, part_recv, out_send, out_recv,
):
    a = lax.axis_index("ctx")
    c = lax.axis_index("clu")
    t = lax.axis_index("tp")
    k = lax.rem(t, 2)
    y = t // 2
    pair = c // 2
    side = lax.rem(c, 2)
    near = side != pair
    count = tok_ref.shape[0]
    half = tok_ref.shape[1] // 2
    run = half // 2
    quarter = half // 4
    core_peer = {"tp": y * 2 + 1 - k}
    y_peer = {"tp": (1 - y) * 2 + k}
    x_peer = {"ctx": 1 - a}
    mate = pair * 2 + 1 - side
    twin = (1 - pair) * 2 + side

    def at_clu(index):
        return {"clu": index}

    def remote(src, dst, send, recv, peer):
        return pltpu.make_async_remote_copy(
            src_ref=src, dst_ref=dst, send_sem=send, recv_sem=recv,
            device_id=peer, device_id_type=MESH,
        )

    def kept(q):
        return pl.ds(pl.multiple_of(q * quarter, quarter), quarter)

    def held(which, q):
        start = (q // 2) * half + which * run + lax.rem(q, 2) * quarter
        return pl.ds(pl.multiple_of(start, quarter), quarter)

    def piece(ctx, at):
        return weights.at[:, pl.ds(pl.multiple_of((ctx * 2 + at) * depth, depth), depth)]

    barrier = pltpu.get_barrier_semaphore()
    others = [at_clu(lax.rem(c + d, owners)) for d in range(1, owners)]
    others += [core_peer, y_peer, x_peer]
    for peer in others:
        pl.semaphore_signal(barrier, inc=1, device_id=peer, device_id_type=MESH)
    local = [
        pltpu.make_async_copy(
            tok_ref.at[:, pl.ds(pl.multiple_of(i * half + pair * run, run), run)],
            rows.at[c, :, pl.ds(i * run, run)], own_sem.at[i],
        )
        for i in range(2)
    ]
    local.append(pltpu.make_async_copy(w_ref.at[side], piece(a, side), own_sem.at[2]))
    local.append(pltpu.make_async_copy(cl_ref.at[c], ids.at[c], own_sem.at[3]))
    for copy in local:
        copy.start()
    pl.semaphore_wait(barrier, len(others))

    blocks = [
        (1 - pair) * 2 + pair,
        (1 - pair) * 2 + 1 - pair,
        mate,
    ]

    def cross():
        turn = jnp.where(near, 0, 1)
        return remote(
            tok_ref.at[:, held(1 - pair, t)], rows.at[c, :, kept(t)],
            cross_send.at[0], cross_recv.at[turn], at_clu(2 - pair),
        )

    def cross_came(n):
        here = rows.at[blocks[n], :, kept(t)]
        return remote(here, here, cross_send.at[0], cross_recv.at[n], at_clu(mate))

    def forward(n):
        here = rows.at[blocks[n], :, kept(t)]
        return remote(here, here, fwd_send.at[n], fwd_recv.at[n], at_clu(mate))

    def to_mate():
        return remote(
            tok_ref.at[:, held(pair, t)], rows.at[c, :, kept(t)],
            mate_send.at[0], mate_recv.at[0], at_clu(mate),
        )

    def mate_came():
        here = rows.at[mate, :, kept(t)]
        return remote(here, here, mate_send.at[0], mate_recv.at[0], at_clu(mate))

    def shared(n, q, send, recv, peer):
        here = rows.at[blocks[n], :, kept(q)]
        return remote(here, here, send.at[n], recv.at[n], peer)

    def to_core(n, q):
        return shared(n, q, core_send, core_recv, core_peer)

    def to_y(n, q):
        return shared(n, q, y_send, y_recv, y_peer)

    def to_core_far(n, q):
        return shared(n, q, far_send, far_recv, core_peer)

    def w_mate():
        return remote(w_ref.at[1 - side], piece(a, side), wm_send.at[0], wm_recv.at[0], at_clu(mate))

    def w_mate_came():
        here = piece(a, 1 - side)
        return remote(here, here, wm_send.at[0], wm_recv.at[0], at_clu(mate))

    def w_cross(i, ctx):
        here = piece(ctx, side if i == 0 else 1 - side)
        return remote(w_ref.at[side] if i == 0 else here, here, wx_send.at[i], wx_recv.at[i], x_peer)

    def id_hop(d):
        goal = lax.rem(c + d, owners)
        return remote(cl_ref.at[goal], ids.at[c], id_send.at[d - 1], id_recv.at[d - 1], at_clu(goal))

    def id_came(d):
        source = lax.rem(c + owners - d, owners)
        return remote(ids.at[source], ids.at[source], id_send.at[d - 1], id_recv.at[d - 1], at_clu(source))

    def part_hop(block):
        return remote(part.at[block], theirs.at[block], part_send.at[block], part_recv.at[block], at_clu(twin))

    cross().start()
    w_cross(0, a).start()
    w_mate().start()
    to_mate().start()
    for d in range(1, owners):
        id_hop(d).start()

    def share(n):
        to_y(n, t).start()
        to_core(n, t).start()

    def relay(n):
        q = (1 - y) * 2 + k
        to_y(n, q).wait_recv()
        to_core_far(n, q).start()

    def arrive_near(n):
        cross_came(n).wait_recv()
        forward(n).start()
        share(n)

    def arrive_far(n):
        forward(n).wait_recv()
        share(n)

    def project(block):
        held_rows = rows[block]
        given = jnp.dot(held_rows, weights[1 - pair], preferred_element_type=jnp.float32)
        part[block] = given.astype(jnp.bfloat16)
        part_hop(block).start()
        mine[block] = jnp.dot(held_rows, weights[pair], preferred_element_type=jnp.float32)

    def finish(n):
        to_core(n, y * 2 + 1 - k).wait_recv()
        to_core_far(n, (1 - y) * 2 + 1 - k).wait_recv()
        project(blocks[n])

    pl.when(near)(lambda: arrive_near(0))
    w_mate_came().wait_recv()
    w_cross(1, a).start()
    mate_came().wait_recv()
    share(2)
    pl.when(jnp.logical_not(near))(lambda: arrive_far(0))
    pl.when(near)(lambda: arrive_near(1))
    relay(2)
    for copy in local:
        copy.wait()
    for i in range(2):
        w_cross(i, 1 - a).wait_recv()
    project(c)
    finish(2)
    relay(0)
    pl.when(jnp.logical_not(near))(lambda: arrive_far(1))
    finish(0)
    relay(1)
    finish(1)
    for d in range(1, owners):
        id_came(d).wait_recv()
    for block in range(owners):
        part_hop(block).wait_recv()
        proj[block] = (mine[block] + theirs[block].astype(jnp.float32)).astype(jnp.bfloat16)

    def send_reply(goal):
        return remote(
            reply.at[goal], out_ref.at[:, pl.ds(pl.multiple_of(c * head_dim, head_dim), head_dim)],
            out_send.at[goal], out_recv.at[c], at_clu(goal),
        )

    def keep_reply(goal):
        return pltpu.make_async_copy(
            reply.at[goal], out_ref.at[:, pl.ds(pl.multiple_of(c * head_dim, head_dim), head_dim)],
            out_send.at[goal],
        )

    for goal in reversed(range(owners)):
        query = proj[goal, :, :head_dim]
        query_ids = jnp.transpose(ids[goal])[:, :1]
        parts = []
        for block in range(goal + 1):
            scores = lax.dot_general(
                query, proj[block, :, :head_dim], (((1,), (1,)), ((), ())),
                preferred_element_type=jnp.float32,
            ) * score_scale
            admitted = query_ids == ids[block, :1, :]
            if block == goal:
                at = lax.broadcasted_iota(jnp.int32, (count, count), 0)
                to = lax.broadcasted_iota(jnp.int32, (count, count), 1)
                scores = jnp.where(at == to, -100000.0, scores)
                admitted = admitted & (to <= at)
            parts.append(jnp.where(admitted, scores, -1e30))
        top = functools.reduce(jnp.maximum, [jnp.max(p, axis=1, keepdims=True) for p in parts])
        total = jnp.zeros((count, 1), jnp.float32)
        mixed = jnp.zeros((count, head_dim), jnp.float32)
        for block, piece_scores in enumerate(parts):
            weighed = jnp.exp(piece_scores - top)
            total += jnp.sum(weighed, axis=1, keepdims=True)
            mixed += jnp.dot(
                weighed.astype(jnp.bfloat16), proj[block, :, head_dim:],
                preferred_element_type=jnp.float32,
            )
        reply[goal] = (mixed / total).astype(jnp.bfloat16)
        pl.when(c != goal)(lambda goal=goal: send_reply(goal).start())
        pl.when(c == goal)(lambda goal=goal: keep_reply(goal).start())

    cross().wait_send()
    w_mate().wait_send()
    to_mate().wait_send()
    for i in range(2):
        w_cross(i, a).wait_send()
    for d in range(1, owners):
        id_hop(d).wait_send()
    for n in range(2):
        pl.when(near)(lambda n=n: forward(n).wait_send())
    for n in range(3):
        to_y(n, t).wait_send()
        to_core(n, t).wait_send()
        to_core_far(n, (1 - y) * 2 + k).wait_send()
    for block in range(owners):
        part_hop(block).wait_send()
    for goal in range(owners):
        @pl.when(c != goal)
        def _(goal=goal):
            send_reply(goal).wait_send()
            column = out_ref.at[:, pl.ds(goal * head_dim, head_dim)]
            remote(reply.at[goal], column, out_send.at[goal], out_recv.at[goal], at_clu(goal)).wait_recv()

        pl.when(c == goal)(lambda goal=goal: keep_reply(goal).wait())


def head_body(tokens, proj_weight, clusters):
    row_count, width = tokens.shape[1:]
    owners = lax.axis_size("clu")
    heads_here = clusters.shape[2]
    depth, _, proj_width = proj_weight.shape
    head_dim = proj_width // heads_here
    pieces = (
        proj_weight.reshape(depth, 2, 2, 2, head_dim)
        .transpose(3, 2, 0, 1, 4)
        .reshape(2, 2, depth, 2 * head_dim)
    )
    labels = jnp.broadcast_to(clusters[0].T[:, None, :], (heads_here, 8, row_count))
    steps = owners - 1
    dma = pltpu.SemaphoreType.DMA
    block = (owners, row_count, 2 * head_dim)
    out = pl.pallas_call(
        functools.partial(head_kernel, owners, depth, head_dim, head_dim ** (-0.5)),
        out_shape=jax.ShapeDtypeStruct((row_count, proj_width), jnp.bfloat16),
        in_specs=[pl.BlockSpec(memory_space=pl.ANY)] * 3,
        out_specs=pl.BlockSpec(memory_space=pl.ANY),
        scratch_shapes=[
            pltpu.VMEM((owners, row_count, width // 2), jnp.bfloat16),
            pltpu.VMEM((2, width // 2, 2 * head_dim), jnp.bfloat16),
            pltpu.VMEM((owners, 8, row_count), jnp.int32),
            pltpu.VMEM(block, jnp.float32),
            pltpu.VMEM(block, jnp.bfloat16),
            pltpu.VMEM(block, jnp.bfloat16),
            pltpu.VMEM(block, jnp.bfloat16),
            pltpu.VMEM((owners, row_count, head_dim), jnp.bfloat16),
            dma((4,)),
            dma((1,)), dma((1,)),
            dma((2,)), dma((2,)),
            dma((steps,)), dma((steps,)),
            dma((1,)), dma((2,)),
            dma((2,)), dma((2,)),
            dma((1,)), dma((1,)),
            dma((3,)), dma((3,)),
            dma((3,)), dma((3,)),
            dma((3,)), dma((3,)),
            dma((owners,)), dma((owners,)),
            dma((owners,)), dma((owners,)),
        ],
        compiler_params=pltpu.CompilerParams(
            collective_id=0, has_side_effects=True, vmem_limit_bytes=56 * 1024 * 1024
        ),
    )(tokens[0], pieces, labels)
    return out[None]


def body(tokens, proj_weight, clusters):
    local_rows = tokens[0]
    row_count = local_rows.shape[0]
    owners = lax.axis_size("clu")
    heads_here = clusters.shape[2]
    proj_width = proj_weight.shape[2]
    head_dim = proj_width // heads_here
    capacity = 2 * row_count // owners
    per_owner = CLUSTERS // owners
    length = row_count * owners
    total_slots = owners * capacity
    score_scale = head_dim ** (-0.5)
    weight_piece = lax.all_gather(proj_weight, ("ctx", "clu"), axis=0, tiled=True)
    flat_piece = weight_piece.reshape(weight_piece.shape[0], 2 * proj_width)
    summed = jnp.dot(local_rows, flat_piece, preferred_element_type=jnp.float32)
    projected = summed.astype(jnp.bfloat16)
    queries = projected[:, :proj_width].reshape(row_count, heads_here, head_dim)
    values = projected[:, proj_width:].reshape(row_count, heads_here, head_dim)
    features = jnp.concatenate([queries, values], axis=2).transpose(1, 0, 2)
    cluster_ids = clusters[0]
    owner_of = cluster_ids // per_owner
    onehot = (owner_of[:, :, None] == jnp.arange(owners, dtype=jnp.int32)[None, None, :]).astype(
        jnp.int32
    )
    rank_in = jnp.sum((jnp.cumsum(onehot, axis=0) - onehot) * onehot, axis=2)
    slot_of = (owner_of * capacity + rank_in).T
    head_rows = jnp.arange(heads_here, dtype=jnp.int32)[:, None]
    token_index = jnp.broadcast_to(
        jnp.arange(row_count, dtype=jnp.int32)[None, :], (heads_here, row_count)
    )
    source = jnp.zeros((heads_here, total_slots), jnp.int32).at[head_rows, slot_of].set(token_index)
    positions = lax.axis_index("clu") * row_count + jnp.arange(row_count, dtype=jnp.int32)
    labels = cluster_ids.T * length + positions[None, :]
    slot_tags = (
        jnp.full((heads_here, total_slots), -1, jnp.int32).at[head_rows, slot_of].set(labels)
    )
    outgoing = jnp.take_along_axis(features, source[:, :, None], axis=1)
    outgoing = jnp.where((slot_tags >= 0)[:, :, None], outgoing, jnp.zeros_like(outgoing))
    outgoing = outgoing.reshape(heads_here, owners, capacity, 2 * head_dim)
    slot_tags = slot_tags.reshape(heads_here, owners, capacity)

    def attend_head(head_item):
        slot_block, key_tags = head_item
        flattened = slot_block.reshape(-1, 2 * head_dim)
        key_rows = flattened[:, :head_dim]
        value_rows = flattened[:, head_dim:]
        key_tags = key_tags.reshape(-1)
        scores = (
            jnp.einsum("qd,kd->qk", key_rows, key_rows, preferred_element_type=jnp.float32)
            * score_scale
        )
        tag_group = key_tags // length
        tag_pos = key_tags % length
        admitted = (
            (key_tags[None, :] >= 0)
            & (tag_group[None, :] == tag_group[:, None])
            & (tag_pos[None, :] <= tag_pos[:, None])
        )
        scores = jnp.where(key_tags[None, :] == key_tags[:, None], -100000.0, scores)
        scores = jnp.where(admitted, scores, -1e30)
        row_max = jnp.max(scores, axis=1, keepdims=True)
        exp_scores = jnp.exp(scores - row_max)
        row_total = jnp.sum(exp_scores, axis=1, keepdims=True)
        probabilities = (exp_scores / row_total).astype(jnp.bfloat16)
        result = jnp.dot(probabilities, value_rows, preferred_element_type=jnp.float32).astype(
            jnp.bfloat16
        )
        return result.reshape(slot_block.shape[0], slot_block.shape[1], head_dim)

    replies = lax.map(
        attend_head,
        (
            lax.all_to_all(outgoing, "clu", split_axis=1, concat_axis=1, tiled=True),
            lax.all_to_all(slot_tags, "clu", split_axis=1, concat_axis=1, tiled=True),
        ),
    )
    returned = lax.all_to_all(replies, "clu", split_axis=1, concat_axis=1, tiled=True)
    returned = returned.reshape(heads_here, total_slots, head_dim)
    gathered = jnp.take_along_axis(returned, slot_of[:, :, None], axis=1)
    return gathered.transpose(1, 0, 2).reshape(1, row_count, heads_here * head_dim)


def solution(mesh):
    sizes = dict(mesh.shape)
    heads_here = 16 // sizes["tp"]
    by_head = sizes["ctx"] == 2 and sizes["tp"] == 4 and sizes["clu"] == heads_here == 4
    return jax.shard_map(
        head_body if by_head else body,
        mesh=mesh,
        in_specs=(P("ctx", "clu", None), P(("ctx", "clu"), None, "tp"), P("ctx", "clu", "tp")),
        out_specs=P("ctx", "clu", "tp"),
        check_vma=False,
    )
```

```python
import functools

import jax
import jax.numpy as jnp
from jax import lax
from jax.experimental import pallas as pl
from jax.experimental.pallas import tpu as pltpu
from jax.sharding import PartitionSpec as P

CLUSTERS = 64
MESH = pl.DeviceIdType.MESH


def head_kernel(
    owners, depth, head_dim, score_scale,
    tok_ref, w_ref, cl_ref, out_ref,
    rows, weights, ids, mine, part, theirs, proj, reply,
    own_sem, wm_send, wm_recv, wx_send, wx_recv, id_send, id_recv,
    cross_send, cross_recv, fwd_send, fwd_recv, mate_send, mate_recv,
    core_send, core_recv, y_send, y_recv, far_send, far_recv,
    part_send, part_recv, out_send, out_recv,
):
    a = lax.axis_index("ctx")
    c = lax.axis_index("clu")
    t = lax.axis_index("tp")
    k = lax.rem(t, 2)
    y = t // 2
    pair = c // 2
    side = lax.rem(c, 2)
    near = side != pair
    count = tok_ref.shape[0]
    half = tok_ref.shape[1] // 2
    run = half // 2
    quarter = half // 4
    core_peer = {"tp": y * 2 + 1 - k}
    y_peer = {"tp": (1 - y) * 2 + k}
    x_peer = {"ctx": 1 - a}
    mate = pair * 2 + 1 - side
    twin = (1 - pair) * 2 + side

    def at_clu(index):
        return {"clu": index}

    def remote(src, dst, send, recv, peer):
        return pltpu.make_async_remote_copy(
            src_ref=src, dst_ref=dst, send_sem=send, recv_sem=recv,
            device_id=peer, device_id_type=MESH,
        )

    def kept(q):
        return pl.ds(pl.multiple_of(q * quarter, quarter), quarter)

    def held(which, q):
        start = (q // 2) * half + which * run + lax.rem(q, 2) * quarter
        return pl.ds(pl.multiple_of(start, quarter), quarter)

    heads = (1 - pair, pair)

    def piece(ctx, at, role):
        return weights.at[heads[role], pl.ds(pl.multiple_of((ctx * 2 + at) * depth, depth), depth)]

    def spread(at, role):
        start = pl.multiple_of((heads[role] * 2 + at) * head_dim, head_dim)
        lands = pl.multiple_of((a * 2 + side) * depth, depth)
        return [
            (
                w_ref.at[kind, :, pl.ds(start, head_dim)],
                weights.at[heads[role], pl.ds(lands, depth), pl.ds(kind * head_dim, head_dim)],
            )
            for kind in range(2)
        ]

    barrier = pltpu.get_barrier_semaphore()
    others = [at_clu(lax.rem(c + d, owners)) for d in range(1, owners)]
    others += [core_peer, y_peer, x_peer]
    for peer in others:
        pl.semaphore_signal(barrier, inc=1, device_id=peer, device_id_type=MESH)
    local = [
        pltpu.make_async_copy(
            tok_ref.at[:, pl.ds(pl.multiple_of(i * half + pair * run, run), run)],
            rows.at[c, :, pl.ds(i * run, run)], own_sem.at[i],
        )
        for i in range(2)
    ]
    local.append(pltpu.make_async_copy(cl_ref.at[c], ids.at[c], own_sem.at[2]))
    for copy in local:
        copy.start()
    for role in range(2):
        for src, dst in spread(side, role):
            pltpu.make_async_copy(src, dst, own_sem.at[3 + role]).start()
    pl.semaphore_wait(barrier, len(others))

    blocks = [
        (1 - pair) * 2 + pair,
        (1 - pair) * 2 + 1 - pair,
        mate,
    ]

    def cross():
        turn = jnp.where(near, 0, 1)
        return remote(
            tok_ref.at[:, held(1 - pair, t)], rows.at[c, :, kept(t)],
            cross_send.at[0], cross_recv.at[turn], at_clu(2 - pair),
        )

    def cross_came(n):
        here = rows.at[blocks[n], :, kept(t)]
        return remote(here, here, cross_send.at[0], cross_recv.at[n], at_clu(mate))

    def forward(n):
        here = rows.at[blocks[n], :, kept(t)]
        return remote(here, here, fwd_send.at[n], fwd_recv.at[n], at_clu(mate))

    def to_mate():
        return remote(
            tok_ref.at[:, held(pair, t)], rows.at[c, :, kept(t)],
            mate_send.at[0], mate_recv.at[0], at_clu(mate),
        )

    def mate_came():
        here = rows.at[mate, :, kept(t)]
        return remote(here, here, mate_send.at[0], mate_recv.at[0], at_clu(mate))

    def shared(n, q, send, recv, peer):
        here = rows.at[blocks[n], :, kept(q)]
        return remote(here, here, send.at[n], recv.at[n], peer)

    def to_core(n, q):
        return shared(n, q, core_send, core_recv, core_peer)

    def to_y(n, q):
        return shared(n, q, y_send, y_recv, y_peer)

    def to_core_far(n, q):
        return shared(n, q, far_send, far_recv, core_peer)

    def w_mate(role):
        for src, dst in spread(1 - side, role):
            remote(src, dst, wm_send.at[role], wm_recv.at[role], at_clu(mate)).start()

    def w_mate_all(role):
        here = piece(a, 1 - side, role)
        return remote(here, here, wm_send.at[role], wm_recv.at[role], at_clu(mate))

    def w_cross_own(role):
        for src, dst in spread(side, role):
            remote(src, dst, wx_send.at[0, role], wx_recv.at[0, role], x_peer).start()

    def w_cross(i, ctx, role):
        here = piece(ctx, side if i == 0 else 1 - side, role)
        return remote(here, here, wx_send.at[i, role], wx_recv.at[i, role], x_peer)

    def w_pass(role):
        w_mate_all(role).wait_recv()
        w_cross(1, a, role).start()

    def w_ready(role):
        here = piece(a, side, role)
        pltpu.make_async_copy(here, here, own_sem.at[3 + role]).wait()
        for i in range(2):
            w_cross(i, 1 - a, role).wait_recv()

    def id_hop(d):
        goal = lax.rem(c + d, owners)
        return remote(cl_ref.at[goal], ids.at[c], id_send.at[d - 1], id_recv.at[d - 1], at_clu(goal))

    def id_came(d):
        source = lax.rem(c + owners - d, owners)
        return remote(ids.at[source], ids.at[source], id_send.at[d - 1], id_recv.at[d - 1], at_clu(source))

    def part_hop(block):
        return remote(part.at[block], theirs.at[block], part_send.at[block], part_recv.at[block], at_clu(twin))

    cross().start()
    w_cross_own(0)
    w_mate(0)
    to_mate().start()
    w_cross_own(1)
    pl.when(jnp.logical_not(near))(lambda: w_mate(1))
    for d in range(1, owners):
        id_hop(d).start()

    def share(n):
        to_y(n, t).start()
        to_core(n, t).start()

    def relay(n):
        q = (1 - y) * 2 + k
        to_y(n, q).wait_recv()
        to_core_far(n, q).start()

    def arrive_near(n):
        cross_came(n).wait_recv()
        forward(n).start()
        share(n)

    def arrive_far(n):
        forward(n).wait_recv()
        share(n)

    def give(block):
        given = jnp.dot(rows[block], weights[1 - pair], preferred_element_type=jnp.float32)
        part[block] = given.astype(jnp.bfloat16)
        part_hop(block).start()

    def finish(n):
        to_core(n, y * 2 + 1 - k).wait_recv()
        to_core_far(n, (1 - y) * 2 + 1 - k).wait_recv()
        give(blocks[n])

    pl.when(near)(lambda: arrive_near(0))
    w_pass(0)

    @pl.when(near)
    def _():
        arrive_near(1)
        w_mate(1)

    mate_came().wait_recv()
    share(2)
    pl.when(jnp.logical_not(near))(lambda: arrive_far(0))
    relay(2)
    for copy in local:
        copy.wait()
    w_ready(0)
    give(c)
    finish(2)
    relay(0)
    pl.when(jnp.logical_not(near))(lambda: arrive_far(1))
    w_pass(1)
    finish(0)
    relay(1)
    finish(1)
    w_ready(1)
    for block in range(owners):
        mine[block] = jnp.dot(rows[block], weights[pair], preferred_element_type=jnp.float32)
    for d in range(1, owners):
        id_came(d).wait_recv()
    for block in range(owners):
        part_hop(block).wait_recv()
        proj[block] = (mine[block] + theirs[block].astype(jnp.float32)).astype(jnp.bfloat16)

    def send_reply(goal):
        return remote(
            reply.at[goal], out_ref.at[:, pl.ds(pl.multiple_of(c * head_dim, head_dim), head_dim)],
            out_send.at[goal], out_recv.at[c], at_clu(goal),
        )

    def keep_reply(goal):
        return pltpu.make_async_copy(
            reply.at[goal], out_ref.at[:, pl.ds(pl.multiple_of(c * head_dim, head_dim), head_dim)],
            out_send.at[goal],
        )

    for goal in reversed(range(owners)):
        query = proj[goal, :, :head_dim]
        query_ids = jnp.transpose(ids[goal])[:, :1]
        parts = []
        for block in range(goal + 1):
            scores = lax.dot_general(
                query, proj[block, :, :head_dim], (((1,), (1,)), ((), ())),
                preferred_element_type=jnp.float32,
            ) * score_scale
            admitted = query_ids == ids[block, :1, :]
            if block == goal:
                at = lax.broadcasted_iota(jnp.int32, (count, count), 0)
                to = lax.broadcasted_iota(jnp.int32, (count, count), 1)
                scores = jnp.where(at == to, -100000.0, scores)
                admitted = admitted & (to <= at)
            parts.append(jnp.where(admitted, scores, -1e30))
        top = functools.reduce(jnp.maximum, [jnp.max(p, axis=1, keepdims=True) for p in parts])
        total = jnp.zeros((count, 1), jnp.float32)
        mixed = jnp.zeros((count, head_dim), jnp.float32)
        for block, piece_scores in enumerate(parts):
            weighed = jnp.exp(piece_scores - top)
            total += jnp.sum(weighed, axis=1, keepdims=True)
            mixed += jnp.dot(
                weighed.astype(jnp.bfloat16), proj[block, :, head_dim:],
                preferred_element_type=jnp.float32,
            )
        reply[goal] = (mixed / total).astype(jnp.bfloat16)
        pl.when(c != goal)(lambda goal=goal: send_reply(goal).start())
        pl.when(c == goal)(lambda goal=goal: keep_reply(goal).start())

    cross().wait_send()
    to_mate().wait_send()
    for role in range(2):
        w_mate_all(role).wait_send()
        for i in range(2):
            w_cross(i, a, role).wait_send()
    for d in range(1, owners):
        id_hop(d).wait_send()
    for n in range(2):
        pl.when(near)(lambda n=n: forward(n).wait_send())
    for n in range(3):
        to_y(n, t).wait_send()
        to_core(n, t).wait_send()
        to_core_far(n, (1 - y) * 2 + k).wait_send()
    for block in range(owners):
        part_hop(block).wait_send()
    for goal in range(owners):
        @pl.when(c != goal)
        def _(goal=goal):
            send_reply(goal).wait_send()
            column = out_ref.at[:, pl.ds(goal * head_dim, head_dim)]
            remote(reply.at[goal], column, out_send.at[goal], out_recv.at[goal], at_clu(goal)).wait_recv()

        pl.when(c == goal)(lambda goal=goal: keep_reply(goal).wait())


def head_body(tokens, proj_weight, clusters):
    row_count, width = tokens.shape[1:]
    owners = lax.axis_size("clu")
    heads_here = clusters.shape[2]
    depth, _, proj_width = proj_weight.shape
    head_dim = proj_width // heads_here
    kinds = proj_weight.transpose(1, 0, 2)
    labels = jnp.broadcast_to(clusters[0].T[:, None, :], (heads_here, 8, row_count))
    steps = owners - 1
    dma = pltpu.SemaphoreType.DMA
    block = (owners, row_count, 2 * head_dim)
    out = pl.pallas_call(
        functools.partial(head_kernel, owners, depth, head_dim, head_dim ** (-0.5)),
        out_shape=jax.ShapeDtypeStruct((row_count, proj_width), jnp.bfloat16),
        in_specs=[pl.BlockSpec(memory_space=space) for space in (pltpu.HBM, pl.ANY, pl.ANY)],
        out_specs=pl.BlockSpec(memory_space=pl.ANY),
        scratch_shapes=[
            pltpu.VMEM((owners, row_count, width // 2), jnp.bfloat16),
            pltpu.VMEM((2, width // 2, 2 * head_dim), jnp.bfloat16),
            pltpu.VMEM((owners, 8, row_count), jnp.int32),
            pltpu.VMEM(block, jnp.float32),
            pltpu.VMEM(block, jnp.bfloat16),
            pltpu.VMEM(block, jnp.bfloat16),
            pltpu.VMEM(block, jnp.bfloat16),
            pltpu.VMEM((owners, row_count, head_dim), jnp.bfloat16),
            dma((5,)),
            dma((2,)), dma((2,)),
            dma((2, 2)), dma((2, 2)),
            dma((steps,)), dma((steps,)),
            dma((1,)), dma((2,)),
            dma((2,)), dma((2,)),
            dma((1,)), dma((1,)),
            dma((3,)), dma((3,)),
            dma((3,)), dma((3,)),
            dma((3,)), dma((3,)),
            dma((owners,)), dma((owners,)),
            dma((owners,)), dma((owners,)),
        ],
        compiler_params=pltpu.CompilerParams(
            collective_id=0, has_side_effects=True, vmem_limit_bytes=40 * 1024 * 1024
        ),
    )(tokens[0], kinds, labels)
    return out[None]


def body(tokens, proj_weight, clusters):
    local_rows = tokens[0]
    row_count = local_rows.shape[0]
    owners = lax.axis_size("clu")
    heads_here = clusters.shape[2]
    proj_width = proj_weight.shape[2]
    head_dim = proj_width // heads_here
    capacity = 2 * row_count // owners
    per_owner = CLUSTERS // owners
    length = row_count * owners
    total_slots = owners * capacity
    score_scale = head_dim ** (-0.5)
    weight_piece = lax.all_gather(proj_weight, ("ctx", "clu"), axis=0, tiled=True)
    flat_piece = weight_piece.reshape(weight_piece.shape[0], 2 * proj_width)
    summed = jnp.dot(local_rows, flat_piece, preferred_element_type=jnp.float32)
    projected = summed.astype(jnp.bfloat16)
    queries = projected[:, :proj_width].reshape(row_count, heads_here, head_dim)
    values = projected[:, proj_width:].reshape(row_count, heads_here, head_dim)
    features = jnp.concatenate([queries, values], axis=2).transpose(1, 0, 2)
    cluster_ids = clusters[0]
    owner_of = cluster_ids // per_owner
    onehot = (owner_of[:, :, None] == jnp.arange(owners, dtype=jnp.int32)[None, None, :]).astype(
        jnp.int32
    )
    rank_in = jnp.sum((jnp.cumsum(onehot, axis=0) - onehot) * onehot, axis=2)
    slot_of = (owner_of * capacity + rank_in).T
    head_rows = jnp.arange(heads_here, dtype=jnp.int32)[:, None]
    token_index = jnp.broadcast_to(
        jnp.arange(row_count, dtype=jnp.int32)[None, :], (heads_here, row_count)
    )
    source = jnp.zeros((heads_here, total_slots), jnp.int32).at[head_rows, slot_of].set(token_index)
    positions = lax.axis_index("clu") * row_count + jnp.arange(row_count, dtype=jnp.int32)
    labels = cluster_ids.T * length + positions[None, :]
    slot_tags = (
        jnp.full((heads_here, total_slots), -1, jnp.int32).at[head_rows, slot_of].set(labels)
    )
    outgoing = jnp.take_along_axis(features, source[:, :, None], axis=1)
    outgoing = jnp.where((slot_tags >= 0)[:, :, None], outgoing, jnp.zeros_like(outgoing))
    outgoing = outgoing.reshape(heads_here, owners, capacity, 2 * head_dim)
    slot_tags = slot_tags.reshape(heads_here, owners, capacity)

    def attend_head(head_item):
        slot_block, key_tags = head_item
        flattened = slot_block.reshape(-1, 2 * head_dim)
        key_rows = flattened[:, :head_dim]
        value_rows = flattened[:, head_dim:]
        key_tags = key_tags.reshape(-1)
        scores = (
            jnp.einsum("qd,kd->qk", key_rows, key_rows, preferred_element_type=jnp.float32)
            * score_scale
        )
        tag_group = key_tags // length
        tag_pos = key_tags % length
        admitted = (
            (key_tags[None, :] >= 0)
            & (tag_group[None, :] == tag_group[:, None])
            & (tag_pos[None, :] <= tag_pos[:, None])
        )
        scores = jnp.where(key_tags[None, :] == key_tags[:, None], -100000.0, scores)
        scores = jnp.where(admitted, scores, -1e30)
        row_max = jnp.max(scores, axis=1, keepdims=True)
        exp_scores = jnp.exp(scores - row_max)
        row_total = jnp.sum(exp_scores, axis=1, keepdims=True)
        probabilities = (exp_scores / row_total).astype(jnp.bfloat16)
        result = jnp.dot(probabilities, value_rows, preferred_element_type=jnp.float32).astype(
            jnp.bfloat16
        )
        return result.reshape(slot_block.shape[0], slot_block.shape[1], head_dim)

    replies = lax.map(
        attend_head,
        (
            lax.all_to_all(outgoing, "clu", split_axis=1, concat_axis=1, tiled=True),
            lax.all_to_all(slot_tags, "clu", split_axis=1, concat_axis=1, tiled=True),
        ),
    )
    returned = lax.all_to_all(replies, "clu", split_axis=1, concat_axis=1, tiled=True)
    returned = returned.reshape(heads_here, total_slots, head_dim)
    gathered = jnp.take_along_axis(returned, slot_of[:, :, None], axis=1)
    return gathered.transpose(1, 0, 2).reshape(1, row_count, heads_here * head_dim)


def solution(mesh):
    sizes = dict(mesh.shape)
    heads_here = 16 // sizes["tp"]
    by_head = sizes["ctx"] == 2 and sizes["tp"] == 4 and sizes["clu"] == heads_here == 4
    return jax.shard_map(
        head_body if by_head else body,
        mesh=mesh,
        in_specs=(P("ctx", "clu", None), P(("ctx", "clu"), None, "tp"), P("ctx", "clu", "tp")),
        out_specs=P("ctx", "clu", "tp"),
        check_vma=False,
    )
```

```python
import functools

import jax
import jax.numpy as jnp
from jax import lax
from jax.experimental import pallas as pl
from jax.experimental.pallas import tpu as pltpu
from jax.sharding import PartitionSpec as P

CLUSTERS = 64
MESH = pl.DeviceIdType.MESH


def head_kernel(
    owners, depth, head_dim, score_scale,
    tok_ref, w_ref, cl_ref, out_ref,
    rows, weights, ids, mine, part, theirs, proj, reply,
    own_sem, wm_send, wm_recv, wx_send, wx_recv, id_send, id_recv,
    cross_send, cross_recv, fwd_send, fwd_recv, mate_send, mate_recv,
    core_send, core_recv, y_send, y_recv, far_send, far_recv,
    part_send, part_recv, out_send, out_recv,
):
    a = lax.axis_index("ctx")
    c = lax.axis_index("clu")
    t = lax.axis_index("tp")
    k = lax.rem(t, 2)
    y = t // 2
    pair = c // 2
    side = lax.rem(c, 2)
    near = side != pair
    count = tok_ref.shape[0]
    half = tok_ref.shape[1] // 2
    run = half // 2
    quarter = half // 4
    core_peer = {"tp": y * 2 + 1 - k}
    y_peer = {"tp": (1 - y) * 2 + k}
    x_peer = {"ctx": 1 - a}
    mate = pair * 2 + 1 - side
    twin = (1 - pair) * 2 + side

    def at_clu(index):
        return {"clu": index}

    def remote(src, dst, send, recv, peer):
        return pltpu.make_async_remote_copy(
            src_ref=src, dst_ref=dst, send_sem=send, recv_sem=recv,
            device_id=peer, device_id_type=MESH,
        )

    def kept(q):
        return pl.ds(pl.multiple_of(q * quarter, quarter), quarter)

    def held(which, q):
        start = (q // 2) * half + which * run + lax.rem(q, 2) * quarter
        return pl.ds(pl.multiple_of(start, quarter), quarter)

    heads = (1 - pair, pair)

    def piece(ctx, at, role):
        return weights.at[heads[role], pl.ds(pl.multiple_of((ctx * 2 + at) * depth, depth), depth)]

    def spread(at, role):
        start = pl.multiple_of((heads[role] * 2 + at) * head_dim, head_dim)
        lands = pl.multiple_of((a * 2 + side) * depth, depth)
        return [
            (
                w_ref.at[kind, :, pl.ds(start, head_dim)],
                weights.at[heads[role], pl.ds(lands, depth), pl.ds(kind * head_dim, head_dim)],
            )
            for kind in range(2)
        ]

    barrier = pltpu.get_barrier_semaphore()
    others = [at_clu(lax.rem(c + d, owners)) for d in range(1, owners)]
    others += [core_peer, y_peer, x_peer]
    for peer in others:
        pl.semaphore_signal(barrier, inc=1, device_id=peer, device_id_type=MESH)
    local = [
        pltpu.make_async_copy(
            tok_ref.at[:, pl.ds(pl.multiple_of(i * half + pair * run, run), run)],
            rows.at[c, :, pl.ds(i * run, run)], own_sem.at[i],
        )
        for i in range(2)
    ]
    local.append(pltpu.make_async_copy(cl_ref.at[c], ids.at[c], own_sem.at[2]))
    for copy in local:
        copy.start()
    for role in range(2):
        for src, dst in spread(side, role):
            pltpu.make_async_copy(src, dst, own_sem.at[3 + role]).start()
    pl.semaphore_wait(barrier, len(others))

    blocks = [
        (1 - pair) * 2 + pair,
        (1 - pair) * 2 + 1 - pair,
        mate,
    ]

    def cross():
        turn = jnp.where(near, 0, 1)
        return remote(
            tok_ref.at[:, held(1 - pair, t)], rows.at[c, :, kept(t)],
            cross_send.at[0], cross_recv.at[turn], at_clu(2 - pair),
        )

    def cross_came(n):
        here = rows.at[blocks[n], :, kept(t)]
        return remote(here, here, cross_send.at[0], cross_recv.at[n], at_clu(mate))

    def forward(n):
        here = rows.at[blocks[n], :, kept(t)]
        return remote(here, here, fwd_send.at[n], fwd_recv.at[n], at_clu(mate))

    def to_mate():
        return remote(
            tok_ref.at[:, held(pair, t)], rows.at[c, :, kept(t)],
            mate_send.at[0], mate_recv.at[0], at_clu(mate),
        )

    def mate_came():
        here = rows.at[mate, :, kept(t)]
        return remote(here, here, mate_send.at[0], mate_recv.at[0], at_clu(mate))

    def shared(n, q, send, recv, peer):
        here = rows.at[blocks[n], :, kept(q)]
        return remote(here, here, send.at[n], recv.at[n], peer)

    def to_core(n, q):
        return shared(n, q, core_send, core_recv, core_peer)

    def to_y(n, q):
        return shared(n, q, y_send, y_recv, y_peer)

    def to_core_far(n, q):
        return shared(n, q, far_send, far_recv, core_peer)

    def w_mate(role):
        for src, dst in spread(1 - side, role):
            remote(src, dst, wm_send.at[role], wm_recv.at[role], at_clu(mate)).start()

    def w_mate_all(role):
        here = piece(a, 1 - side, role)
        return remote(here, here, wm_send.at[role], wm_recv.at[role], at_clu(mate))

    def w_cross_own(role):
        for src, dst in spread(side, role):
            remote(src, dst, wx_send.at[0, role], wx_recv.at[0, role], x_peer).start()

    def w_cross(i, ctx, role):
        here = piece(ctx, side if i == 0 else 1 - side, role)
        return remote(here, here, wx_send.at[i, role], wx_recv.at[i, role], x_peer)

    def w_pass(role):
        w_mate_all(role).wait_recv()
        w_cross(1, a, role).start()

    def w_ready(role):
        here = piece(a, side, role)
        pltpu.make_async_copy(here, here, own_sem.at[3 + role]).wait()
        for i in range(2):
            w_cross(i, 1 - a, role).wait_recv()

    def id_hop(d):
        goal = lax.rem(c + d, owners)
        return remote(cl_ref.at[goal], ids.at[c], id_send.at[d - 1], id_recv.at[d - 1], at_clu(goal))

    def id_came(d):
        source = lax.rem(c + owners - d, owners)
        return remote(ids.at[source], ids.at[source], id_send.at[d - 1], id_recv.at[d - 1], at_clu(source))

    def part_hop(block):
        return remote(part.at[block], theirs.at[block], part_send.at[block], part_recv.at[block], at_clu(twin))

    def share(n):
        to_y(n, t).start()
        to_core(n, t).start()

    def relay(n):
        q = (1 - y) * 2 + k
        to_y(n, q).wait_recv()
        to_core_far(n, q).start()

    def arrive_near(n):
        cross_came(n).wait_recv()
        forward(n).start()
        share(n)

    def arrive_far(n):
        forward(n).wait_recv()
        share(n)

    def give(block):
        given = jnp.dot(rows[block], weights[1 - pair], preferred_element_type=jnp.float32)
        part[block] = given.astype(jnp.bfloat16)
        part_hop(block).start()

    def finish(n):
        to_core(n, y * 2 + 1 - k).wait_recv()
        to_core_far(n, (1 - y) * 2 + 1 - k).wait_recv()
        give(blocks[n])

    cross().start()
    w_cross_own(0)
    w_mate(0)
    pl.when(near)(lambda: to_mate().start())
    w_cross_own(1)
    for d in range(1, owners):
        id_hop(d).start()
    for copy in local:
        copy.wait()

    @pl.when(near)
    def _():
        arrive_near(0)
        w_pass(0)
        arrive_near(1)
        relay(0)
        mate_came().wait_recv()
        share(2)
        relay(1)
        w_ready(0)
        give(c)
        finish(0)
        finish(1)
        for n in range(2):
            forward(n).wait_send()
        w_mate(1)
        w_pass(1)
        relay(2)
        finish(2)
        cross().wait_send()
        w_mate_all(0).wait_send()

    @pl.when(jnp.logical_not(near))
    def _():
        cross().wait_send()
        to_mate().start()
        w_pass(0)
        w_mate_all(0).wait_send()
        w_mate(1)
        mate_came().wait_recv()
        share(2)
        arrive_far(0)
        relay(2)
        w_ready(0)
        give(c)
        finish(2)
        arrive_far(1)
        relay(0)
        finish(0)
        w_pass(1)
        relay(1)
        finish(1)

    w_ready(1)
    for block in range(owners):
        mine[block] = jnp.dot(rows[block], weights[pair], preferred_element_type=jnp.float32)
    for d in range(1, owners):
        id_came(d).wait_recv()
    for block in range(owners):
        part_hop(block).wait_recv()
        proj[block] = (mine[block] + theirs[block].astype(jnp.float32)).astype(jnp.bfloat16)

    def send_reply(goal):
        return remote(
            reply.at[goal], out_ref.at[:, pl.ds(pl.multiple_of(c * head_dim, head_dim), head_dim)],
            out_send.at[goal], out_recv.at[c], at_clu(goal),
        )

    def keep_reply(goal):
        return pltpu.make_async_copy(
            reply.at[goal], out_ref.at[:, pl.ds(pl.multiple_of(c * head_dim, head_dim), head_dim)],
            out_send.at[goal],
        )

    for goal in reversed(range(owners)):
        query = proj[goal, :, :head_dim]
        query_ids = jnp.transpose(ids[goal])[:, :1]
        parts = []
        for block in range(goal + 1):
            scores = lax.dot_general(
                query, proj[block, :, :head_dim], (((1,), (1,)), ((), ())),
                preferred_element_type=jnp.float32,
            ) * score_scale
            admitted = query_ids == ids[block, :1, :]
            if block == goal:
                at = lax.broadcasted_iota(jnp.int32, (count, count), 0)
                to = lax.broadcasted_iota(jnp.int32, (count, count), 1)
                scores = jnp.where(at == to, -100000.0, scores)
                admitted = admitted & (to <= at)
            parts.append(jnp.where(admitted, scores, -1e30))
        top = functools.reduce(jnp.maximum, [jnp.max(p, axis=1, keepdims=True) for p in parts])
        total = jnp.zeros((count, 1), jnp.float32)
        mixed = jnp.zeros((count, head_dim), jnp.float32)
        for block, piece_scores in enumerate(parts):
            weighed = jnp.exp(piece_scores - top)
            total += jnp.sum(weighed, axis=1, keepdims=True)
            mixed += jnp.dot(
                weighed.astype(jnp.bfloat16), proj[block, :, head_dim:],
                preferred_element_type=jnp.float32,
            )
        reply[goal] = (mixed / total).astype(jnp.bfloat16)
        pl.when(c != goal)(lambda goal=goal: send_reply(goal).start())
        pl.when(c == goal)(lambda goal=goal: keep_reply(goal).start())

    to_mate().wait_send()
    w_mate_all(1).wait_send()
    for role in range(2):
        for i in range(2):
            w_cross(i, a, role).wait_send()
    for d in range(1, owners):
        id_hop(d).wait_send()
    for n in range(3):
        to_y(n, t).wait_send()
        to_core(n, t).wait_send()
        to_core_far(n, (1 - y) * 2 + k).wait_send()
    for block in range(owners):
        part_hop(block).wait_send()
    for goal in range(owners):
        @pl.when(c != goal)
        def _(goal=goal):
            send_reply(goal).wait_send()
            column = out_ref.at[:, pl.ds(goal * head_dim, head_dim)]
            remote(reply.at[goal], column, out_send.at[goal], out_recv.at[goal], at_clu(goal)).wait_recv()

        pl.when(c == goal)(lambda goal=goal: keep_reply(goal).wait())


def head_body(tokens, proj_weight, clusters):
    row_count, width = tokens.shape[1:]
    owners = lax.axis_size("clu")
    heads_here = clusters.shape[2]
    depth, _, proj_width = proj_weight.shape
    head_dim = proj_width // heads_here
    kinds = proj_weight.transpose(1, 0, 2)
    labels = jnp.broadcast_to(clusters[0].T[:, None, :], (heads_here, 8, row_count))
    steps = owners - 1
    dma = pltpu.SemaphoreType.DMA
    block = (owners, row_count, 2 * head_dim)
    out = pl.pallas_call(
        functools.partial(head_kernel, owners, depth, head_dim, head_dim ** (-0.5)),
        out_shape=jax.ShapeDtypeStruct((row_count, proj_width), jnp.bfloat16),
        in_specs=[pl.BlockSpec(memory_space=space) for space in (pltpu.HBM, pl.ANY, pl.ANY)],
        out_specs=pl.BlockSpec(memory_space=pl.ANY),
        scratch_shapes=[
            pltpu.VMEM((owners, row_count, width // 2), jnp.bfloat16),
            pltpu.VMEM((2, width // 2, 2 * head_dim), jnp.bfloat16),
            pltpu.VMEM((owners, 8, row_count), jnp.int32),
            pltpu.VMEM(block, jnp.float32),
            pltpu.VMEM(block, jnp.bfloat16),
            pltpu.VMEM(block, jnp.bfloat16),
            pltpu.VMEM(block, jnp.bfloat16),
            pltpu.VMEM((owners, row_count, head_dim), jnp.bfloat16),
            dma((5,)),
            dma((2,)), dma((2,)),
            dma((2, 2)), dma((2, 2)),
            dma((steps,)), dma((steps,)),
            dma((1,)), dma((2,)),
            dma((2,)), dma((2,)),
            dma((1,)), dma((1,)),
            dma((3,)), dma((3,)),
            dma((3,)), dma((3,)),
            dma((3,)), dma((3,)),
            dma((owners,)), dma((owners,)),
            dma((owners,)), dma((owners,)),
        ],
        compiler_params=pltpu.CompilerParams(
            collective_id=0, has_side_effects=True, vmem_limit_bytes=40 * 1024 * 1024
        ),
    )(tokens[0], kinds, labels)
    return out[None]


def body(tokens, proj_weight, clusters):
    local_rows = tokens[0]
    row_count = local_rows.shape[0]
    owners = lax.axis_size("clu")
    heads_here = clusters.shape[2]
    proj_width = proj_weight.shape[2]
    head_dim = proj_width // heads_here
    capacity = 2 * row_count // owners
    per_owner = CLUSTERS // owners
    length = row_count * owners
    total_slots = owners * capacity
    score_scale = head_dim ** (-0.5)
    weight_piece = lax.all_gather(proj_weight, ("ctx", "clu"), axis=0, tiled=True)
    flat_piece = weight_piece.reshape(weight_piece.shape[0], 2 * proj_width)
    summed = jnp.dot(local_rows, flat_piece, preferred_element_type=jnp.float32)
    projected = summed.astype(jnp.bfloat16)
    queries = projected[:, :proj_width].reshape(row_count, heads_here, head_dim)
    values = projected[:, proj_width:].reshape(row_count, heads_here, head_dim)
    features = jnp.concatenate([queries, values], axis=2).transpose(1, 0, 2)
    cluster_ids = clusters[0]
    owner_of = cluster_ids // per_owner
    onehot = (owner_of[:, :, None] == jnp.arange(owners, dtype=jnp.int32)[None, None, :]).astype(
        jnp.int32
    )
    rank_in = jnp.sum((jnp.cumsum(onehot, axis=0) - onehot) * onehot, axis=2)
    slot_of = (owner_of * capacity + rank_in).T
    head_rows = jnp.arange(heads_here, dtype=jnp.int32)[:, None]
    token_index = jnp.broadcast_to(
        jnp.arange(row_count, dtype=jnp.int32)[None, :], (heads_here, row_count)
    )
    source = jnp.zeros((heads_here, total_slots), jnp.int32).at[head_rows, slot_of].set(token_index)
    positions = lax.axis_index("clu") * row_count + jnp.arange(row_count, dtype=jnp.int32)
    labels = cluster_ids.T * length + positions[None, :]
    slot_tags = (
        jnp.full((heads_here, total_slots), -1, jnp.int32).at[head_rows, slot_of].set(labels)
    )
    outgoing = jnp.take_along_axis(features, source[:, :, None], axis=1)
    outgoing = jnp.where((slot_tags >= 0)[:, :, None], outgoing, jnp.zeros_like(outgoing))
    outgoing = outgoing.reshape(heads_here, owners, capacity, 2 * head_dim)
    slot_tags = slot_tags.reshape(heads_here, owners, capacity)

    def attend_head(head_item):
        slot_block, key_tags = head_item
        flattened = slot_block.reshape(-1, 2 * head_dim)
        key_rows = flattened[:, :head_dim]
        value_rows = flattened[:, head_dim:]
        key_tags = key_tags.reshape(-1)
        scores = (
            jnp.einsum("qd,kd->qk", key_rows, key_rows, preferred_element_type=jnp.float32)
            * score_scale
        )
        tag_group = key_tags // length
        tag_pos = key_tags % length
        admitted = (
            (key_tags[None, :] >= 0)
            & (tag_group[None, :] == tag_group[:, None])
            & (tag_pos[None, :] <= tag_pos[:, None])
        )
        scores = jnp.where(key_tags[None, :] == key_tags[:, None], -100000.0, scores)
        scores = jnp.where(admitted, scores, -1e30)
        row_max = jnp.max(scores, axis=1, keepdims=True)
        exp_scores = jnp.exp(scores - row_max)
        row_total = jnp.sum(exp_scores, axis=1, keepdims=True)
        probabilities = (exp_scores / row_total).astype(jnp.bfloat16)
        result = jnp.dot(probabilities, value_rows, preferred_element_type=jnp.float32).astype(
            jnp.bfloat16
        )
        return result.reshape(slot_block.shape[0], slot_block.shape[1], head_dim)

    replies = lax.map(
        attend_head,
        (
            lax.all_to_all(outgoing, "clu", split_axis=1, concat_axis=1, tiled=True),
            lax.all_to_all(slot_tags, "clu", split_axis=1, concat_axis=1, tiled=True),
        ),
    )
    returned = lax.all_to_all(replies, "clu", split_axis=1, concat_axis=1, tiled=True)
    returned = returned.reshape(heads_here, total_slots, head_dim)
    gathered = jnp.take_along_axis(returned, slot_of[:, :, None], axis=1)
    return gathered.transpose(1, 0, 2).reshape(1, row_count, heads_here * head_dim)


def solution(mesh):
    sizes = dict(mesh.shape)
    heads_here = 16 // sizes["tp"]
    by_head = sizes["ctx"] == 2 and sizes["tp"] == 4 and sizes["clu"] == heads_here == 4
    return jax.shard_map(
        head_body if by_head else body,
        mesh=mesh,
        in_specs=(P("ctx", "clu", None), P(("ctx", "clu"), None, "tp"), P("ctx", "clu", "tp")),
        out_specs=P("ctx", "clu", "tp"),
        check_vma=False,
    )
```

```python
import functools

import jax
import jax.numpy as jnp
from jax import lax
from jax.experimental import pallas as pl
from jax.experimental.pallas import tpu as pltpu
from jax.sharding import PartitionSpec as P

CLUSTERS = 64
MESH = pl.DeviceIdType.MESH


def head_kernel(
    owners, depth, head_dim, score_scale,
    tok_ref, w_ref, cl_ref, out_ref,
    rows, weights, stage, ids, mine, part, theirs, proj, reply,
    own_sem, wm_send, wm_recv, wx_send, wx_recv, id_send, id_recv,
    cross_send, cross_recv, fwd_send, fwd_recv, mate_send, mate_recv,
    core_send, core_recv, y_send, y_recv, far_send, far_recv,
    part_send, part_recv, out_send, out_recv,
):
    a = lax.axis_index("ctx")
    c = lax.axis_index("clu")
    t = lax.axis_index("tp")
    k = lax.rem(t, 2)
    y = t // 2
    pair = c // 2
    side = lax.rem(c, 2)
    near = side != pair
    count = tok_ref.shape[0]
    half = tok_ref.shape[1] // 2
    run = half // 2
    quarter = half // 4
    core_peer = {"tp": y * 2 + 1 - k}
    y_peer = {"tp": (1 - y) * 2 + k}
    x_peer = {"ctx": 1 - a}
    mate = pair * 2 + 1 - side
    twin = (1 - pair) * 2 + side

    def at_clu(index):
        return {"clu": index}

    def remote(src, dst, send, recv, peer):
        return pltpu.make_async_remote_copy(
            src_ref=src, dst_ref=dst, send_sem=send, recv_sem=recv,
            device_id=peer, device_id_type=MESH,
        )

    def held(which, q):
        start = (q // 2) * half + which * run + lax.rem(q, 2) * quarter
        return pl.ds(pl.multiple_of(start, quarter), quarter)

    heads = (1 - pair, pair)

    def piece(ctx, at, role):
        return weights.at[heads[role], pl.ds(pl.multiple_of((ctx * 2 + at) * depth, depth), depth)]

    barrier = pltpu.get_barrier_semaphore()
    others = [at_clu(lax.rem(c + d, owners)) for d in range(1, owners)]
    others += [core_peer, y_peer, x_peer]
    for peer in others:
        pl.semaphore_signal(barrier, inc=1, device_id=peer, device_id_type=MESH)
    local = [
        pltpu.make_async_copy(tok_ref.at[:, held(pair, q)], rows.at[c, q], own_sem.at[q])
        for q in range(4)
    ]
    local.append(pltpu.make_async_copy(cl_ref.at[c], ids.at[c], own_sem.at[4]))
    for copy in local:
        copy.start()
    for role in range(2):
        for kind in range(2):
            lands = pl.ds(kind * head_dim, head_dim)
            start = pl.multiple_of((heads[role] * 2 + side) * head_dim, head_dim)
            mine_at = pl.ds(pl.multiple_of((a * 2 + side) * depth, depth), depth)
            weights[heads[role], mine_at, lands] = w_ref[kind, :, pl.ds(start, head_dim)]
            start = pl.multiple_of((heads[role] * 2 + 1 - side) * head_dim, head_dim)
            stage[role, :, lands] = w_ref[kind, :, pl.ds(start, head_dim)]
    pl.semaphore_wait(barrier, len(others))

    blocks = [
        (1 - pair) * 2 + pair,
        (1 - pair) * 2 + 1 - pair,
        mate,
    ]

    def cross():
        turn = jnp.where(near, 0, 1)
        return remote(
            tok_ref.at[:, held(1 - pair, t)], rows.at[c, t],
            cross_send.at[0], cross_recv.at[turn], at_clu(2 - pair),
        )

    def cross_came(n):
        here = rows.at[blocks[n], t]
        return remote(here, here, cross_send.at[0], cross_recv.at[n], at_clu(mate))

    def forward(n):
        here = rows.at[blocks[n], t]
        return remote(here, here, fwd_send.at[n], fwd_recv.at[n], at_clu(mate))

    def to_mate():
        return remote(
            tok_ref.at[:, held(pair, t)], rows.at[c, t],
            mate_send.at[0], mate_recv.at[0], at_clu(mate),
        )

    def mate_came():
        here = rows.at[mate, t]
        return remote(here, here, mate_send.at[0], mate_recv.at[0], at_clu(mate))

    def shared(n, q, send, recv, peer):
        here = rows.at[blocks[n], q]
        return remote(here, here, send.at[n], recv.at[n], peer)

    def to_core(n, q):
        return shared(n, q, core_send, core_recv, core_peer)

    def to_y(n, q):
        return shared(n, q, y_send, y_recv, y_peer)

    def to_core_far(n, q):
        return shared(n, q, far_send, far_recv, core_peer)

    def w_mate(role):
        return remote(
            stage.at[role], piece(a, side, role), wm_send.at[role], wm_recv.at[role], at_clu(mate)
        )

    def w_mate_came(role):
        here = piece(a, 1 - side, role)
        return remote(here, here, wm_send.at[role], wm_recv.at[role], at_clu(mate))

    def w_cross(i, ctx, role):
        here = piece(ctx, side if i == 0 else 1 - side, role)
        return remote(here, here, wx_send.at[i, role], wx_recv.at[i, role], x_peer)

    def w_pass(role):
        w_mate_came(role).wait_recv()
        w_cross(1, a, role).start()

    def w_ready(role):
        for i in range(2):
            w_cross(i, 1 - a, role).wait_recv()

    def id_hop(d):
        goal = lax.rem(c + d, owners)
        return remote(cl_ref.at[goal], ids.at[c], id_send.at[d - 1], id_recv.at[d - 1], at_clu(goal))

    def id_came(d):
        source = lax.rem(c + owners - d, owners)
        return remote(ids.at[source], ids.at[source], id_send.at[d - 1], id_recv.at[d - 1], at_clu(source))

    def part_hop(block):
        return remote(part.at[block], theirs.at[block], part_send.at[block], part_recv.at[block], at_clu(twin))

    cross().start()
    w_cross(0, a, 0).start()
    w_mate(0).start()
    to_mate().start()
    w_cross(0, a, 1).start()
    pl.when(jnp.logical_not(near))(lambda: w_mate(1).start())
    for d in range(1, owners):
        id_hop(d).start()

    def share(n):
        to_y(n, t).start()
        to_core(n, t).start()

    def relay(n):
        q = (1 - y) * 2 + k
        to_y(n, q).wait_recv()
        to_core_far(n, q).start()

    def arrive_near(n):
        cross_came(n).wait_recv()
        forward(n).start()
        share(n)

    def arrive_far(n):
        forward(n).wait_recv()
        share(n)

    def whole(block):
        return jnp.concatenate([rows[block, q] for q in range(4)], axis=1)

    def give(block):
        given = jnp.dot(whole(block), weights[1 - pair], preferred_element_type=jnp.float32)
        part[block] = given.astype(jnp.bfloat16)
        part_hop(block).start()

    def finish(n):
        to_core(n, y * 2 + 1 - k).wait_recv()
        to_core_far(n, (1 - y) * 2 + 1 - k).wait_recv()
        give(blocks[n])

    pl.when(near)(lambda: arrive_near(0))
    w_pass(0)

    @pl.when(near)
    def _():
        arrive_near(1)
        w_mate(1).start()

    mate_came().wait_recv()
    share(2)
    pl.when(jnp.logical_not(near))(lambda: arrive_far(0))
    relay(2)
    for copy in local:
        copy.wait()
    w_ready(0)
    give(c)
    finish(2)
    relay(0)
    pl.when(jnp.logical_not(near))(lambda: arrive_far(1))
    w_pass(1)
    finish(0)
    relay(1)
    finish(1)
    w_ready(1)
    for block in range(owners):
        mine[block] = jnp.dot(whole(block), weights[pair], preferred_element_type=jnp.float32)
    for d in range(1, owners):
        id_came(d).wait_recv()
    for block in range(owners):
        part_hop(block).wait_recv()
        proj[block] = (mine[block] + theirs[block].astype(jnp.float32)).astype(jnp.bfloat16)

    def send_reply(goal):
        return remote(
            reply.at[goal], out_ref.at[:, pl.ds(pl.multiple_of(c * head_dim, head_dim), head_dim)],
            out_send.at[goal], out_recv.at[c], at_clu(goal),
        )

    def keep_reply(goal):
        return pltpu.make_async_copy(
            reply.at[goal], out_ref.at[:, pl.ds(pl.multiple_of(c * head_dim, head_dim), head_dim)],
            out_send.at[goal],
        )

    for goal in reversed(range(owners)):
        query = proj[goal, :, :head_dim]
        query_ids = jnp.transpose(ids[goal])[:, :1]
        parts = []
        for block in range(goal + 1):
            scores = lax.dot_general(
                query, proj[block, :, :head_dim], (((1,), (1,)), ((), ())),
                preferred_element_type=jnp.float32,
            ) * score_scale
            admitted = query_ids == ids[block, :1, :]
            if block == goal:
                at = lax.broadcasted_iota(jnp.int32, (count, count), 0)
                to = lax.broadcasted_iota(jnp.int32, (count, count), 1)
                scores = jnp.where(at == to, -100000.0, scores)
                admitted = admitted & (to <= at)
            parts.append(jnp.where(admitted, scores, -1e30))
        top = functools.reduce(jnp.maximum, [jnp.max(p, axis=1, keepdims=True) for p in parts])
        total = jnp.zeros((count, 1), jnp.float32)
        mixed = jnp.zeros((count, head_dim), jnp.float32)
        for block, piece_scores in enumerate(parts):
            weighed = jnp.exp(piece_scores - top)
            total += jnp.sum(weighed, axis=1, keepdims=True)
            mixed += jnp.dot(
                weighed.astype(jnp.bfloat16), proj[block, :, head_dim:],
                preferred_element_type=jnp.float32,
            )
        reply[goal] = (mixed / total).astype(jnp.bfloat16)
        pl.when(c != goal)(lambda goal=goal: send_reply(goal).start())
        pl.when(c == goal)(lambda goal=goal: keep_reply(goal).start())

    cross().wait_send()
    to_mate().wait_send()
    for role in range(2):
        w_mate(role).wait_send()
        for i in range(2):
            w_cross(i, a, role).wait_send()
    for d in range(1, owners):
        id_hop(d).wait_send()
    for n in range(2):
        pl.when(near)(lambda n=n: forward(n).wait_send())
    for n in range(3):
        to_y(n, t).wait_send()
        to_core(n, t).wait_send()
        to_core_far(n, (1 - y) * 2 + k).wait_send()
    for block in range(owners):
        part_hop(block).wait_send()
    for goal in range(owners):
        @pl.when(c != goal)
        def _(goal=goal):
            send_reply(goal).wait_send()
            column = out_ref.at[:, pl.ds(goal * head_dim, head_dim)]
            remote(reply.at[goal], column, out_send.at[goal], out_recv.at[goal], at_clu(goal)).wait_recv()

        pl.when(c == goal)(lambda goal=goal: keep_reply(goal).wait())


def head_body(tokens, proj_weight, clusters):
    row_count, width = tokens.shape[1:]
    owners = lax.axis_size("clu")
    heads_here = clusters.shape[2]
    depth, _, proj_width = proj_weight.shape
    head_dim = proj_width // heads_here
    kinds = proj_weight.transpose(1, 0, 2)
    labels = jnp.broadcast_to(clusters[0].T[:, None, :], (heads_here, 8, row_count))
    steps = owners - 1
    dma = pltpu.SemaphoreType.DMA
    block = (owners, row_count, 2 * head_dim)
    out = pl.pallas_call(
        functools.partial(head_kernel, owners, depth, head_dim, head_dim ** (-0.5)),
        out_shape=jax.ShapeDtypeStruct((row_count, proj_width), jnp.bfloat16),
        in_specs=[pl.BlockSpec(memory_space=space) for space in (pl.ANY, pltpu.VMEM, pl.ANY)],
        out_specs=pl.BlockSpec(memory_space=pl.ANY),
        scratch_shapes=[
            pltpu.VMEM((owners, 4, row_count, width // 8), jnp.bfloat16),
            pltpu.VMEM((2, width // 2, 2 * head_dim), jnp.bfloat16),
            pltpu.VMEM((2, depth, 2 * head_dim), jnp.bfloat16),
            pltpu.VMEM((owners, 8, row_count), jnp.int32),
            pltpu.VMEM(block, jnp.float32),
            pltpu.VMEM(block, jnp.bfloat16),
            pltpu.VMEM(block, jnp.bfloat16),
            pltpu.VMEM(block, jnp.bfloat16),
            pltpu.VMEM((owners, row_count, head_dim), jnp.bfloat16),
            dma((5,)),
            dma((2,)), dma((2,)),
            dma((2, 2)), dma((2, 2)),
            dma((steps,)), dma((steps,)),
            dma((1,)), dma((2,)),
            dma((2,)), dma((2,)),
            dma((1,)), dma((1,)),
            dma((3,)), dma((3,)),
            dma((3,)), dma((3,)),
            dma((3,)), dma((3,)),
            dma((owners,)), dma((owners,)),
            dma((owners,)), dma((owners,)),
        ],
        compiler_params=pltpu.CompilerParams(
            collective_id=0, has_side_effects=True, vmem_limit_bytes=40 * 1024 * 1024
        ),
    )(tokens[0], kinds, labels)
    return out[None]


def body(tokens, proj_weight, clusters):
    local_rows = tokens[0]
    row_count = local_rows.shape[0]
    owners = lax.axis_size("clu")
    heads_here = clusters.shape[2]
    proj_width = proj_weight.shape[2]
    head_dim = proj_width // heads_here
    capacity = 2 * row_count // owners
    per_owner = CLUSTERS // owners
    length = row_count * owners
    total_slots = owners * capacity
    score_scale = head_dim ** (-0.5)
    weight_piece = lax.all_gather(proj_weight, ("ctx", "clu"), axis=0, tiled=True)
    flat_piece = weight_piece.reshape(weight_piece.shape[0], 2 * proj_width)
    summed = jnp.dot(local_rows, flat_piece, preferred_element_type=jnp.float32)
    projected = summed.astype(jnp.bfloat16)
    queries = projected[:, :proj_width].reshape(row_count, heads_here, head_dim)
    values = projected[:, proj_width:].reshape(row_count, heads_here, head_dim)
    features = jnp.concatenate([queries, values], axis=2).transpose(1, 0, 2)
    cluster_ids = clusters[0]
    owner_of = cluster_ids // per_owner
    onehot = (owner_of[:, :, None] == jnp.arange(owners, dtype=jnp.int32)[None, None, :]).astype(
        jnp.int32
    )
    rank_in = jnp.sum((jnp.cumsum(onehot, axis=0) - onehot) * onehot, axis=2)
    slot_of = (owner_of * capacity + rank_in).T
    head_rows = jnp.arange(heads_here, dtype=jnp.int32)[:, None]
    token_index = jnp.broadcast_to(
        jnp.arange(row_count, dtype=jnp.int32)[None, :], (heads_here, row_count)
    )
    source = jnp.zeros((heads_here, total_slots), jnp.int32).at[head_rows, slot_of].set(token_index)
    positions = lax.axis_index("clu") * row_count + jnp.arange(row_count, dtype=jnp.int32)
    labels = cluster_ids.T * length + positions[None, :]
    slot_tags = (
        jnp.full((heads_here, total_slots), -1, jnp.int32).at[head_rows, slot_of].set(labels)
    )
    outgoing = jnp.take_along_axis(features, source[:, :, None], axis=1)
    outgoing = jnp.where((slot_tags >= 0)[:, :, None], outgoing, jnp.zeros_like(outgoing))
    outgoing = outgoing.reshape(heads_here, owners, capacity, 2 * head_dim)
    slot_tags = slot_tags.reshape(heads_here, owners, capacity)

    def attend_head(head_item):
        slot_block, key_tags = head_item
        flattened = slot_block.reshape(-1, 2 * head_dim)
        key_rows = flattened[:, :head_dim]
        value_rows = flattened[:, head_dim:]
        key_tags = key_tags.reshape(-1)
        scores = (
            jnp.einsum("qd,kd->qk", key_rows, key_rows, preferred_element_type=jnp.float32)
            * score_scale
        )
        tag_group = key_tags // length
        tag_pos = key_tags % length
        admitted = (
            (key_tags[None, :] >= 0)
            & (tag_group[None, :] == tag_group[:, None])
            & (tag_pos[None, :] <= tag_pos[:, None])
        )
        scores = jnp.where(key_tags[None, :] == key_tags[:, None], -100000.0, scores)
        scores = jnp.where(admitted, scores, -1e30)
        row_max = jnp.max(scores, axis=1, keepdims=True)
        exp_scores = jnp.exp(scores - row_max)
        row_total = jnp.sum(exp_scores, axis=1, keepdims=True)
        probabilities = (exp_scores / row_total).astype(jnp.bfloat16)
        result = jnp.dot(probabilities, value_rows, preferred_element_type=jnp.float32).astype(
            jnp.bfloat16
        )
        return result.reshape(slot_block.shape[0], slot_block.shape[1], head_dim)

    replies = lax.map(
        attend_head,
        (
            lax.all_to_all(outgoing, "clu", split_axis=1, concat_axis=1, tiled=True),
            lax.all_to_all(slot_tags, "clu", split_axis=1, concat_axis=1, tiled=True),
        ),
    )
    returned = lax.all_to_all(replies, "clu", split_axis=1, concat_axis=1, tiled=True)
    returned = returned.reshape(heads_here, total_slots, head_dim)
    gathered = jnp.take_along_axis(returned, slot_of[:, :, None], axis=1)
    return gathered.transpose(1, 0, 2).reshape(1, row_count, heads_here * head_dim)


def solution(mesh):
    sizes = dict(mesh.shape)
    heads_here = 16 // sizes["tp"]
    by_head = sizes["ctx"] == 2 and sizes["tp"] == 4 and sizes["clu"] == heads_here == 4
    return jax.shard_map(
        head_body if by_head else body,
        mesh=mesh,
        in_specs=(P("ctx", "clu", None), P(("ctx", "clu"), None, "tp"), P("ctx", "clu", "tp")),
        out_specs=P("ctx", "clu", "tp"),
        check_vma=False,
    )
```

```python
import functools

import jax
import jax.numpy as jnp
from jax import lax
from jax.experimental import pallas as pl
from jax.experimental.pallas import tpu as pltpu
from jax.sharding import PartitionSpec as P

CLUSTERS = 64
LOG2E = 1.4426950408889634
MESH = pl.DeviceIdType.MESH


def head_kernel(
    owners, depth, head_dim, score_scale,
    tok_ref, w_ref, cl_ref, out_ref,
    rows, weights, stage, ids, mine, part, theirs, proj, reply,
    own_sem, wm_send, wm_recv, wx_send, wx_recv, id_send, id_recv,
    cross_send, cross_recv, fwd_send, fwd_recv, mate_send, mate_recv,
    core_send, core_recv, y_send, y_recv, far_send, far_recv,
    part_send, part_recv, out_send, out_recv,
):
    a = lax.axis_index("ctx")
    c = lax.axis_index("clu")
    t = lax.axis_index("tp")
    k = lax.rem(t, 2)
    y = t // 2
    pair = c // 2
    side = lax.rem(c, 2)
    near = side != pair
    count = tok_ref.shape[0]
    short = count // 2
    cut = depth // 2
    half = tok_ref.shape[1] // 2
    run = half // 2
    quarter = half // 4
    core_peer = {"tp": y * 2 + 1 - k}
    y_peer = {"tp": (1 - y) * 2 + k}
    x_peer = {"ctx": 1 - a}
    mate = pair * 2 + 1 - side
    twin = (1 - pair) * 2 + side

    def at_clu(index):
        return {"clu": index}

    def remote(src, dst, send, recv, peer):
        return pltpu.make_async_remote_copy(
            src_ref=src, dst_ref=dst, send_sem=send, recv_sem=recv,
            device_id=peer, device_id_type=MESH,
        )

    def held(which, q):
        start = (q // 2) * half + which * run + lax.rem(q, 2) * quarter
        return pl.ds(pl.multiple_of(start, quarter), quarter)

    heads = (1 - pair, pair)

    def piece(ctx, at, role, e):
        start = pl.multiple_of((ctx * 2 + at) * depth + e * cut, cut)
        return weights.at[heads[role], pl.ds(start, cut)]

    barrier = pltpu.get_barrier_semaphore()
    others = [at_clu(lax.rem(c + d, owners)) for d in range(1, owners)]
    others += [core_peer, y_peer, x_peer]
    for peer in others:
        pl.semaphore_signal(barrier, inc=1, device_id=peer, device_id_type=MESH)
    local = [
        pltpu.make_async_copy(
            tok_ref.at[pl.ds(h * short, short), held(pair, q)], rows.at[c, h, q], own_sem.at[h * 4 + q]
        )
        for q in range(4) for h in range(2)
    ]
    local.append(pltpu.make_async_copy(cl_ref.at[c], ids.at[c], own_sem.at[8]))
    for copy in local:
        copy.start()
    for role in range(2):
        for kind in range(2):
            lands = pl.ds(kind * head_dim, head_dim)
            start = pl.multiple_of((heads[role] * 2 + side) * head_dim, head_dim)
            mine_at = pl.ds(pl.multiple_of((a * 2 + side) * depth, depth), depth)
            weights[heads[role], mine_at, lands] = w_ref[kind, :, pl.ds(start, head_dim)]
            start = pl.multiple_of((heads[role] * 2 + 1 - side) * head_dim, head_dim)
            stage[role, :, lands] = w_ref[kind, :, pl.ds(start, head_dim)]
    pl.semaphore_wait(barrier, len(others))

    blocks = [
        (1 - pair) * 2 + pair,
        (1 - pair) * 2 + 1 - pair,
        mate,
    ]

    def cross(h):
        turn = jnp.where(near, 0, 1)
        return remote(
            tok_ref.at[pl.ds(h * short, short), held(1 - pair, t)], rows.at[c, h, t],
            cross_send.at[h], cross_recv.at[turn, h], at_clu(2 - pair),
        )

    def cross_came(n, h):
        here = rows.at[blocks[n], h, t]
        return remote(here, here, cross_send.at[h], cross_recv.at[n, h], at_clu(mate))

    def forward(n, h):
        here = rows.at[blocks[n], h, t]
        return remote(here, here, fwd_send.at[n, h], fwd_recv.at[n, h], at_clu(mate))

    def to_mate(h):
        return remote(
            tok_ref.at[pl.ds(h * short, short), held(pair, t)], rows.at[c, h, t],
            mate_send.at[h], mate_recv.at[h], at_clu(mate),
        )

    def mate_came(h):
        here = rows.at[mate, h, t]
        return remote(here, here, mate_send.at[h], mate_recv.at[h], at_clu(mate))

    def shared(n, h, q, send, recv, peer):
        here = rows.at[blocks[n], h, q]
        return remote(here, here, send.at[n, h], recv.at[n, h], peer)

    def to_core(n, h, q):
        return shared(n, h, q, core_send, core_recv, core_peer)

    def to_y(n, h, q):
        return shared(n, h, q, y_send, y_recv, y_peer)

    def to_core_far(n, h, q):
        return shared(n, h, q, far_send, far_recv, core_peer)

    def w_mate(role, e):
        return remote(
            stage.at[role, pl.ds(e * cut, cut)], piece(a, side, role, e),
            wm_send.at[role, e], wm_recv.at[role, e], at_clu(mate),
        )

    def w_mate_came(role, e):
        here = piece(a, 1 - side, role, e)
        return remote(here, here, wm_send.at[role, e], wm_recv.at[role, e], at_clu(mate))

    def w_cross(i, ctx, role, e):
        here = piece(ctx, side if i == 0 else 1 - side, role, e)
        return remote(here, here, wx_send.at[i, role, e], wx_recv.at[i, role, e], x_peer)

    def w_pass(role):
        for e in range(2):
            w_mate_came(role, e).wait_recv()
            w_cross(1, a, role, e).start()

    def w_ready(role):
        for i in range(2):
            for e in range(2):
                w_cross(i, 1 - a, role, e).wait_recv()

    def id_hop(d):
        goal = lax.rem(c + d, owners)
        return remote(cl_ref.at[goal], ids.at[c], id_send.at[d - 1], id_recv.at[d - 1], at_clu(goal))

    def id_came(d):
        source = lax.rem(c + owners - d, owners)
        return remote(ids.at[source], ids.at[source], id_send.at[d - 1], id_recv.at[d - 1], at_clu(source))

    def part_hop(block, h):
        return remote(
            part.at[block, h], theirs.at[block, h],
            part_send.at[block, h], part_recv.at[block, h], at_clu(twin),
        )

    for h in range(2):
        cross(h).start()
    for role in range(2):
        for e in range(2):
            w_cross(0, a, role, e).start()
            w_mate(role, e).start()
        if role == 0:
            for h in range(2):
                to_mate(h).start()
    for d in range(1, owners):
        id_hop(d).start()

    def share(n, h):
        to_y(n, h, t).start()
        to_core(n, h, t).start()

    def relay(n):
        q = (1 - y) * 2 + k
        for h in range(2):
            to_y(n, h, q).wait_recv()
            to_core_far(n, h, q).start()

    def arrive_near(n):
        for h in range(2):
            cross_came(n, h).wait_recv()
            forward(n, h).start()
            share(n, h)

    def arrive_far(n):
        for h in range(2):
            forward(n, h).wait_recv()
            share(n, h)

    def whole(block, h):
        return jnp.concatenate([rows[block, h, q] for q in range(4)], axis=1)

    def give(block, h):
        given = jnp.dot(whole(block, h), weights[1 - pair], preferred_element_type=jnp.float32)
        part[block, h] = given.astype(jnp.bfloat16)
        part_hop(block, h).start()

    def finish(n):
        for h in range(2):
            to_core(n, h, y * 2 + 1 - k).wait_recv()
            to_core_far(n, h, (1 - y) * 2 + 1 - k).wait_recv()
            give(blocks[n], h)

    pl.when(near)(lambda: arrive_near(0))
    w_pass(0)
    pl.when(near)(lambda: arrive_near(1))
    for h in range(2):
        mate_came(h).wait_recv()
        share(2, h)
    pl.when(jnp.logical_not(near))(lambda: arrive_far(0))
    relay(2)
    for copy in local:
        copy.wait()
    w_ready(0)
    for h in range(2):
        give(c, h)
    finish(2)
    relay(0)
    w_pass(1)
    finish(0)
    pl.when(jnp.logical_not(near))(lambda: arrive_far(1))
    relay(1)
    finish(1)
    w_ready(1)
    for block in range(owners):
        for h in range(2):
            mine[block, h] = jnp.dot(whole(block, h), weights[pair], preferred_element_type=jnp.float32)
    for d in range(1, owners):
        id_came(d).wait_recv()
    for block in range(owners):
        for h in range(2):
            part_hop(block, h).wait_recv()
            proj[block, h * short : (h + 1) * short] = (
                mine[block, h] + theirs[block, h].astype(jnp.float32)
            ).astype(jnp.bfloat16)

    def send_reply(goal):
        return remote(
            reply.at[goal], out_ref.at[:, pl.ds(pl.multiple_of(c * head_dim, head_dim), head_dim)],
            out_send.at[goal], out_recv.at[c], at_clu(goal),
        )

    def keep_reply(goal):
        return pltpu.make_async_copy(
            reply.at[goal], out_ref.at[:, pl.ds(pl.multiple_of(c * head_dim, head_dim), head_dim)],
            out_send.at[goal],
        )

    for goal in reversed(range(owners)):
        query = proj[goal, :, :head_dim]
        query_ids = jnp.transpose(ids[goal])[:, :1]
        parts = []
        for block in range(goal + 1):
            scores = lax.dot_general(
                query, proj[block, :, :head_dim], (((1,), (1,)), ((), ())),
                preferred_element_type=jnp.float32,
            ) * (score_scale * LOG2E)
            admitted = query_ids == ids[block, :1, :]
            if block == goal:
                at = lax.broadcasted_iota(jnp.int32, (count, count), 0)
                to = lax.broadcasted_iota(jnp.int32, (count, count), 1)
                scores = jnp.where(at == to, -100000.0 * LOG2E, scores)
                admitted = admitted & (to <= at)
            parts.append(jnp.where(admitted, scores, -1e30))
        top = functools.reduce(jnp.maximum, [jnp.max(p, axis=1, keepdims=True) for p in parts])
        total = jnp.zeros((count, 1), jnp.float32)
        mixed = jnp.zeros((count, head_dim), jnp.float32)
        for block, piece_scores in enumerate(parts):
            weighed = jnp.exp2(piece_scores - top)
            total += jnp.sum(weighed, axis=1, keepdims=True)
            mixed += jnp.dot(
                weighed.astype(jnp.bfloat16), proj[block, :, head_dim:],
                preferred_element_type=jnp.float32,
            )
        reply[goal] = (mixed / total).astype(jnp.bfloat16)
        pl.when(c != goal)(lambda goal=goal: send_reply(goal).start())
        pl.when(c == goal)(lambda goal=goal: keep_reply(goal).start())

    for h in range(2):
        cross(h).wait_send()
        to_mate(h).wait_send()
        for n in range(2):
            pl.when(near)(lambda n=n, h=h: forward(n, h).wait_send())
        for n in range(3):
            to_y(n, h, t).wait_send()
            to_core(n, h, t).wait_send()
            to_core_far(n, h, (1 - y) * 2 + k).wait_send()
        for block in range(owners):
            part_hop(block, h).wait_send()
    for role in range(2):
        for e in range(2):
            w_mate(role, e).wait_send()
            for i in range(2):
                w_cross(i, a, role, e).wait_send()
    for d in range(1, owners):
        id_hop(d).wait_send()
    for goal in range(owners):
        @pl.when(c != goal)
        def _(goal=goal):
            send_reply(goal).wait_send()
            column = out_ref.at[:, pl.ds(goal * head_dim, head_dim)]
            remote(reply.at[goal], column, out_send.at[goal], out_recv.at[goal], at_clu(goal)).wait_recv()

        pl.when(c == goal)(lambda goal=goal: keep_reply(goal).wait())


def head_body(tokens, proj_weight, clusters):
    row_count, width = tokens.shape[1:]
    owners = lax.axis_size("clu")
    heads_here = clusters.shape[2]
    depth, _, proj_width = proj_weight.shape
    head_dim = proj_width // heads_here
    kinds = proj_weight.transpose(1, 0, 2)
    labels = jnp.broadcast_to(clusters[0].T[:, None, :], (heads_here, 8, row_count))
    steps = owners - 1
    dma = pltpu.SemaphoreType.DMA
    split = (owners, 2, row_count // 2, 2 * head_dim)
    out = pl.pallas_call(
        functools.partial(head_kernel, owners, depth, head_dim, head_dim ** (-0.5)),
        out_shape=jax.ShapeDtypeStruct((row_count, proj_width), jnp.bfloat16),
        in_specs=[pl.BlockSpec(memory_space=space) for space in (pl.ANY, pltpu.VMEM, pl.ANY)],
        out_specs=pl.BlockSpec(memory_space=pl.ANY),
        scratch_shapes=[
            pltpu.VMEM((owners, 2, 4, row_count // 2, width // 8), jnp.bfloat16),
            pltpu.VMEM((2, width // 2, 2 * head_dim), jnp.bfloat16),
            pltpu.VMEM((2, depth, 2 * head_dim), jnp.bfloat16),
            pltpu.VMEM((owners, 8, row_count), jnp.int32),
            pltpu.VMEM(split, jnp.float32),
            pltpu.VMEM(split, jnp.bfloat16),
            pltpu.VMEM(split, jnp.bfloat16),
            pltpu.VMEM((owners, row_count, 2 * head_dim), jnp.bfloat16),
            pltpu.VMEM((owners, row_count, head_dim), jnp.bfloat16),
            dma((9,)),
            dma((2, 2)), dma((2, 2)),
            dma((2, 2, 2)), dma((2, 2, 2)),
            dma((steps,)), dma((steps,)),
            dma((2,)), dma((2, 2)),
            dma((2, 2)), dma((2, 2)),
            dma((2,)), dma((2,)),
            dma((3, 2)), dma((3, 2)),
            dma((3, 2)), dma((3, 2)),
            dma((3, 2)), dma((3, 2)),
            dma((owners, 2)), dma((owners, 2)),
            dma((owners,)), dma((owners,)),
        ],
        compiler_params=pltpu.CompilerParams(
            collective_id=0, has_side_effects=True, vmem_limit_bytes=40 * 1024 * 1024
        ),
    )(tokens[0], kinds, labels)
    return out[None]


def body(tokens, proj_weight, clusters):
    local_rows = tokens[0]
    row_count = local_rows.shape[0]
    owners = lax.axis_size("clu")
    heads_here = clusters.shape[2]
    proj_width = proj_weight.shape[2]
    head_dim = proj_width // heads_here
    capacity = 2 * row_count // owners
    per_owner = CLUSTERS // owners
    length = row_count * owners
    total_slots = owners * capacity
    score_scale = head_dim ** (-0.5)
    weight_piece = lax.all_gather(proj_weight, ("ctx", "clu"), axis=0, tiled=True)
    flat_piece = weight_piece.reshape(weight_piece.shape[0], 2 * proj_width)
    summed = jnp.dot(local_rows, flat_piece, preferred_element_type=jnp.float32)
    projected = summed.astype(jnp.bfloat16)
    queries = projected[:, :proj_width].reshape(row_count, heads_here, head_dim)
    values = projected[:, proj_width:].reshape(row_count, heads_here, head_dim)
    features = jnp.concatenate([queries, values], axis=2).transpose(1, 0, 2)
    cluster_ids = clusters[0]
    owner_of = cluster_ids // per_owner
    onehot = (owner_of[:, :, None] == jnp.arange(owners, dtype=jnp.int32)[None, None, :]).astype(
        jnp.int32
    )
    rank_in = jnp.sum((jnp.cumsum(onehot, axis=0) - onehot) * onehot, axis=2)
    slot_of = (owner_of * capacity + rank_in).T
    head_rows = jnp.arange(heads_here, dtype=jnp.int32)[:, None]
    token_index = jnp.broadcast_to(
        jnp.arange(row_count, dtype=jnp.int32)[None, :], (heads_here, row_count)
    )
    source = jnp.zeros((heads_here, total_slots), jnp.int32).at[head_rows, slot_of].set(token_index)
    positions = lax.axis_index("clu") * row_count + jnp.arange(row_count, dtype=jnp.int32)
    labels = cluster_ids.T * length + positions[None, :]
    slot_tags = (
        jnp.full((heads_here, total_slots), -1, jnp.int32).at[head_rows, slot_of].set(labels)
    )
    outgoing = jnp.take_along_axis(features, source[:, :, None], axis=1)
    outgoing = jnp.where((slot_tags >= 0)[:, :, None], outgoing, jnp.zeros_like(outgoing))
    outgoing = outgoing.reshape(heads_here, owners, capacity, 2 * head_dim)
    slot_tags = slot_tags.reshape(heads_here, owners, capacity)

    def attend_head(head_item):
        slot_block, key_tags = head_item
        flattened = slot_block.reshape(-1, 2 * head_dim)
        key_rows = flattened[:, :head_dim]
        value_rows = flattened[:, head_dim:]
        key_tags = key_tags.reshape(-1)
        scores = (
            jnp.einsum("qd,kd->qk", key_rows, key_rows, preferred_element_type=jnp.float32)
            * score_scale
        )
        tag_group = key_tags // length
        tag_pos = key_tags % length
        admitted = (
            (key_tags[None, :] >= 0)
            & (tag_group[None, :] == tag_group[:, None])
            & (tag_pos[None, :] <= tag_pos[:, None])
        )
        scores = jnp.where(key_tags[None, :] == key_tags[:, None], -100000.0, scores)
        scores = jnp.where(admitted, scores, -1e30)
        row_max = jnp.max(scores, axis=1, keepdims=True)
        exp_scores = jnp.exp(scores - row_max)
        row_total = jnp.sum(exp_scores, axis=1, keepdims=True)
        probabilities = (exp_scores / row_total).astype(jnp.bfloat16)
        result = jnp.dot(probabilities, value_rows, preferred_element_type=jnp.float32).astype(
            jnp.bfloat16
        )
        return result.reshape(slot_block.shape[0], slot_block.shape[1], head_dim)

    replies = lax.map(
        attend_head,
        (
            lax.all_to_all(outgoing, "clu", split_axis=1, concat_axis=1, tiled=True),
            lax.all_to_all(slot_tags, "clu", split_axis=1, concat_axis=1, tiled=True),
        ),
    )
    returned = lax.all_to_all(replies, "clu", split_axis=1, concat_axis=1, tiled=True)
    returned = returned.reshape(heads_here, total_slots, head_dim)
    gathered = jnp.take_along_axis(returned, slot_of[:, :, None], axis=1)
    return gathered.transpose(1, 0, 2).reshape(1, row_count, heads_here * head_dim)


def solution(mesh):
    sizes = dict(mesh.shape)
    heads_here = 16 // sizes["tp"]
    by_head = sizes["ctx"] == 2 and sizes["tp"] == 4 and sizes["clu"] == heads_here == 4
    return jax.shard_map(
        head_body if by_head else body,
        mesh=mesh,
        in_specs=(P("ctx", "clu", None), P(("ctx", "clu"), None, "tp"), P("ctx", "clu", "tp")),
        out_specs=P("ctx", "clu", "tp"),
        check_vma=False,
    )
```

```python
import functools

import jax
import jax.numpy as jnp
from jax import lax
from jax.experimental import pallas as pl
from jax.experimental.pallas import tpu as pltpu
from jax.sharding import PartitionSpec as P

CLUSTERS = 64
LOG2E = 1.4426950408889634
MESH = pl.DeviceIdType.MESH


def head_kernel(
    owners, depth, head_dim, score_scale,
    tok_ref, w_ref, cl_ref, out_ref,
    rows, weights, stage, ids, mine, part, theirs, proj, reply,
    own_sem, wm_send, wm_recv, wx_send, wx_recv, id_send, id_recv,
    cross_send, cross_recv, fwd_send, fwd_recv, mate_send, mate_recv,
    core_send, core_recv, y_send, y_recv, far_send, far_recv,
    part_send, part_recv, out_send, out_recv,
):
    a = lax.axis_index("ctx")
    c = lax.axis_index("clu")
    t = lax.axis_index("tp")
    k = lax.rem(t, 2)
    y = t // 2
    pair = c // 2
    side = lax.rem(c, 2)
    near = side != pair
    count = tok_ref.shape[0]
    short = count // 2
    cut = depth // 2
    half = tok_ref.shape[1] // 2
    run = half // 2
    quarter = half // 4
    core_peer = {"tp": y * 2 + 1 - k}
    y_peer = {"tp": (1 - y) * 2 + k}
    x_peer = {"ctx": 1 - a}
    mate = pair * 2 + 1 - side
    twin = (1 - pair) * 2 + side

    def at_clu(index):
        return {"clu": index}

    def remote(src, dst, send, recv, peer):
        return pltpu.make_async_remote_copy(
            src_ref=src, dst_ref=dst, send_sem=send, recv_sem=recv,
            device_id=peer, device_id_type=MESH,
        )

    def held(which, q):
        start = (q // 2) * half + which * run + lax.rem(q, 2) * quarter
        return pl.ds(pl.multiple_of(start, quarter), quarter)

    heads = (1 - pair, pair)

    def piece(ctx, at, role, e):
        start = pl.multiple_of((ctx * 2 + at) * depth + e * cut, cut)
        return weights.at[heads[role], pl.ds(start, cut)]

    barrier = pltpu.get_barrier_semaphore()
    others = [at_clu(lax.rem(c + d, owners)) for d in range(1, owners)]
    others += [core_peer, y_peer, x_peer]
    for peer in others:
        pl.semaphore_signal(barrier, inc=1, device_id=peer, device_id_type=MESH)
    local = [
        pltpu.make_async_copy(
            tok_ref.at[pl.ds(h * short, short), held(pair, q)], rows.at[c, h, q], own_sem.at[h * 4 + q]
        )
        for q in range(4) for h in range(2)
    ]
    local.append(pltpu.make_async_copy(cl_ref.at[c], ids.at[c], own_sem.at[8]))
    for copy in local:
        copy.start()
    for role in range(2):
        for kind in range(2):
            lands = pl.ds(kind * head_dim, head_dim)
            start = pl.multiple_of((heads[role] * 2 + side) * head_dim, head_dim)
            mine_at = pl.ds(pl.multiple_of((a * 2 + side) * depth, depth), depth)
            weights[heads[role], mine_at, lands] = w_ref[kind, :, pl.ds(start, head_dim)]
            start = pl.multiple_of((heads[role] * 2 + 1 - side) * head_dim, head_dim)
            stage[role, :, lands] = w_ref[kind, :, pl.ds(start, head_dim)]
    pl.semaphore_wait(barrier, len(others))

    blocks = [
        (1 - pair) * 2 + pair,
        (1 - pair) * 2 + 1 - pair,
        mate,
    ]

    def cross(h):
        turn = jnp.where(near, 0, 1)
        return remote(
            tok_ref.at[pl.ds(h * short, short), held(1 - pair, t)], rows.at[c, h, t],
            cross_send.at[h], cross_recv.at[turn, h], at_clu(2 - pair),
        )

    def cross_came(n, h):
        here = rows.at[blocks[n], h, t]
        return remote(here, here, cross_send.at[h], cross_recv.at[n, h], at_clu(mate))

    def forward(n, h):
        here = rows.at[blocks[n], h, t]
        return remote(here, here, fwd_send.at[n, h], fwd_recv.at[n, h], at_clu(mate))

    def to_mate(h):
        return remote(
            tok_ref.at[pl.ds(h * short, short), held(pair, t)], rows.at[c, h, t],
            mate_send.at[h], mate_recv.at[h], at_clu(mate),
        )

    def mate_came(h):
        here = rows.at[mate, h, t]
        return remote(here, here, mate_send.at[h], mate_recv.at[h], at_clu(mate))

    def shared(n, h, q, send, recv, peer):
        here = rows.at[blocks[n], h, q]
        return remote(here, here, send.at[n, h], recv.at[n, h], peer)

    def to_core(n, h, q):
        return shared(n, h, q, core_send, core_recv, core_peer)

    def to_y(n, h, q):
        return shared(n, h, q, y_send, y_recv, y_peer)

    def to_core_far(n, h, q):
        return shared(n, h, q, far_send, far_recv, core_peer)

    def w_mate(role, e):
        return remote(
            stage.at[role, pl.ds(e * cut, cut)], piece(a, side, role, e),
            wm_send.at[role, e], wm_recv.at[role, e], at_clu(mate),
        )

    def w_mate_came(role, e):
        here = piece(a, 1 - side, role, e)
        return remote(here, here, wm_send.at[role, e], wm_recv.at[role, e], at_clu(mate))

    def w_cross(i, ctx, role, e):
        here = piece(ctx, side if i == 0 else 1 - side, role, e)
        return remote(here, here, wx_send.at[i, role, e], wx_recv.at[i, role, e], x_peer)

    def w_pass(role):
        for e in range(2):
            w_mate_came(role, e).wait_recv()
            w_cross(1, a, role, e).start()

    def w_ready(role):
        for i in range(2):
            for e in range(2):
                w_cross(i, 1 - a, role, e).wait_recv()

    def id_hop(d):
        goal = lax.rem(c + d, owners)
        return remote(cl_ref.at[goal], ids.at[c], id_send.at[d - 1], id_recv.at[d - 1], at_clu(goal))

    def id_came(d):
        source = lax.rem(c + owners - d, owners)
        return remote(ids.at[source], ids.at[source], id_send.at[d - 1], id_recv.at[d - 1], at_clu(source))

    def part_hop(block, h):
        return remote(
            part.at[block, h], theirs.at[block, h],
            part_send.at[block, h], part_recv.at[block, h], at_clu(twin),
        )

    for h in range(2):
        cross(h).start()
    for role in range(2):
        for e in range(2):
            w_cross(0, a, role, e).start()
            if role == 0:
                w_mate(role, e).start()
        if role == 0:
            for h in range(2):
                to_mate(h).start()
    for d in range(1, owners):
        id_hop(d).start()

    def share(n, h):
        to_y(n, h, t).start()
        to_core(n, h, t).start()

    def relay(n):
        q = (1 - y) * 2 + k
        for h in range(2):
            to_y(n, h, q).wait_recv()
            to_core_far(n, h, q).start()

    def arrive_near(n):
        for h in range(2):
            cross_came(n, h).wait_recv()
            forward(n, h).start()
            share(n, h)

    def arrive_far(n):
        for h in range(2):
            forward(n, h).wait_recv()
            share(n, h)

    def whole(block, h):
        return jnp.concatenate([rows[block, h, q] for q in range(4)], axis=1)

    def give(block, h):
        given = jnp.dot(whole(block, h), weights[1 - pair], preferred_element_type=jnp.float32)
        part[block, h] = given.astype(jnp.bfloat16)
        part_hop(block, h).start()

    def finish(n):
        for h in range(2):
            to_core(n, h, y * 2 + 1 - k).wait_recv()
            to_core_far(n, h, (1 - y) * 2 + 1 - k).wait_recv()
            give(blocks[n], h)

    pl.when(near)(lambda: arrive_near(0))
    w_pass(0)
    pl.when(near)(lambda: arrive_near(1))
    for e in range(2):
        w_mate(1, e).start()
    for h in range(2):
        mate_came(h).wait_recv()
        share(2, h)
    pl.when(jnp.logical_not(near))(lambda: arrive_far(0))
    relay(2)
    for copy in local:
        copy.wait()
    w_ready(0)
    for h in range(2):
        give(c, h)
    finish(2)
    relay(0)
    w_pass(1)
    finish(0)
    pl.when(jnp.logical_not(near))(lambda: arrive_far(1))
    relay(1)
    finish(1)
    w_ready(1)
    for block in range(owners):
        both = jnp.concatenate([whole(block, h) for h in range(2)], axis=0)
        mine[block] = jnp.dot(both, weights[pair], preferred_element_type=jnp.float32)
    for d in range(1, owners):
        id_came(d).wait_recv()
    for block in range(owners):
        for h in range(2):
            part_hop(block, h).wait_recv()
            proj[block, h * short : (h + 1) * short] = (
                mine[block, h * short : (h + 1) * short] + theirs[block, h].astype(jnp.float32)
            ).astype(jnp.bfloat16)

    def send_reply(goal):
        return remote(
            reply.at[goal], out_ref.at[:, pl.ds(pl.multiple_of(c * head_dim, head_dim), head_dim)],
            out_send.at[goal], out_recv.at[c], at_clu(goal),
        )

    def keep_reply(goal):
        return pltpu.make_async_copy(
            reply.at[goal], out_ref.at[:, pl.ds(pl.multiple_of(c * head_dim, head_dim), head_dim)],
            out_send.at[goal],
        )

    for goal in reversed(range(owners)):
        query = proj[goal, :, :head_dim]
        query_ids = jnp.transpose(ids[goal])[:, :1]
        parts = []
        for block in range(goal + 1):
            scores = lax.dot_general(
                query, proj[block, :, :head_dim], (((1,), (1,)), ((), ())),
                preferred_element_type=jnp.float32,
            ) * (score_scale * LOG2E)
            admitted = query_ids == ids[block, :1, :]
            if block == goal:
                at = lax.broadcasted_iota(jnp.int32, (count, count), 0)
                to = lax.broadcasted_iota(jnp.int32, (count, count), 1)
                scores = jnp.where(at == to, -100000.0 * LOG2E, scores)
                admitted = admitted & (to <= at)
            parts.append(jnp.where(admitted, scores, -1e30))
        top = functools.reduce(jnp.maximum, [jnp.max(p, axis=1, keepdims=True) for p in parts])
        total = jnp.zeros((count, 1), jnp.float32)
        mixed = jnp.zeros((count, head_dim), jnp.float32)
        for block, piece_scores in enumerate(parts):
            weighed = jnp.exp2(piece_scores - top)
            total += jnp.sum(weighed, axis=1, keepdims=True)
            mixed += jnp.dot(
                weighed.astype(jnp.bfloat16), proj[block, :, head_dim:],
                preferred_element_type=jnp.float32,
            )
        reply[goal] = (mixed / total).astype(jnp.bfloat16)
        pl.when(c != goal)(lambda goal=goal: send_reply(goal).start())
        pl.when(c == goal)(lambda goal=goal: keep_reply(goal).start())

    for h in range(2):
        cross(h).wait_send()
        to_mate(h).wait_send()
        for n in range(2):
            pl.when(near)(lambda n=n, h=h: forward(n, h).wait_send())
        for n in range(3):
            to_y(n, h, t).wait_send()
            to_core(n, h, t).wait_send()
            to_core_far(n, h, (1 - y) * 2 + k).wait_send()
        for block in range(owners):
            part_hop(block, h).wait_send()
    for role in range(2):
        for e in range(2):
            w_mate(role, e).wait_send()
            for i in range(2):
                w_cross(i, a, role, e).wait_send()
    for d in range(1, owners):
        id_hop(d).wait_send()
    for goal in range(owners):
        @pl.when(c != goal)
        def _(goal=goal):
            send_reply(goal).wait_send()
            column = out_ref.at[:, pl.ds(goal * head_dim, head_dim)]
            remote(reply.at[goal], column, out_send.at[goal], out_recv.at[goal], at_clu(goal)).wait_recv()

        pl.when(c == goal)(lambda goal=goal: keep_reply(goal).wait())


def head_body(tokens, proj_weight, clusters):
    row_count, width = tokens.shape[1:]
    owners = lax.axis_size("clu")
    heads_here = clusters.shape[2]
    depth, _, proj_width = proj_weight.shape
    head_dim = proj_width // heads_here
    kinds = proj_weight.transpose(1, 0, 2)
    labels = jnp.broadcast_to(clusters[0].T[:, None, :], (heads_here, 8, row_count))
    steps = owners - 1
    dma = pltpu.SemaphoreType.DMA
    split = (owners, 2, row_count // 2, 2 * head_dim)
    out = pl.pallas_call(
        functools.partial(head_kernel, owners, depth, head_dim, head_dim ** (-0.5)),
        out_shape=jax.ShapeDtypeStruct((row_count, proj_width), jnp.bfloat16),
        in_specs=[pl.BlockSpec(memory_space=space) for space in (pl.ANY, pltpu.VMEM, pl.ANY)],
        out_specs=pl.BlockSpec(memory_space=pl.ANY),
        scratch_shapes=[
            pltpu.VMEM((owners, 2, 4, row_count // 2, width // 8), jnp.bfloat16),
            pltpu.VMEM((2, width // 2, 2 * head_dim), jnp.bfloat16),
            pltpu.VMEM((2, depth, 2 * head_dim), jnp.bfloat16),
            pltpu.VMEM((owners, 8, row_count), jnp.int32),
            pltpu.VMEM((owners, row_count, 2 * head_dim), jnp.float32),
            pltpu.VMEM(split, jnp.bfloat16),
            pltpu.VMEM(split, jnp.bfloat16),
            pltpu.VMEM((owners, row_count, 2 * head_dim), jnp.bfloat16),
            pltpu.VMEM((owners, row_count, head_dim), jnp.bfloat16),
            dma((9,)),
            dma((2, 2)), dma((2, 2)),
            dma((2, 2, 2)), dma((2, 2, 2)),
            dma((steps,)), dma((steps,)),
            dma((2,)), dma((2, 2)),
            dma((2, 2)), dma((2, 2)),
            dma((2,)), dma((2,)),
            dma((3, 2)), dma((3, 2)),
            dma((3, 2)), dma((3, 2)),
            dma((3, 2)), dma((3, 2)),
            dma((owners, 2)), dma((owners, 2)),
            dma((owners,)), dma((owners,)),
        ],
        compiler_params=pltpu.CompilerParams(
            collective_id=0, has_side_effects=True, vmem_limit_bytes=40 * 1024 * 1024
        ),
    )(tokens[0], kinds, labels)
    return out[None]


def body(tokens, proj_weight, clusters):
    local_rows = tokens[0]
    row_count = local_rows.shape[0]
    owners = lax.axis_size("clu")
    heads_here = clusters.shape[2]
    proj_width = proj_weight.shape[2]
    head_dim = proj_width // heads_here
    capacity = 2 * row_count // owners
    per_owner = CLUSTERS // owners
    length = row_count * owners
    total_slots = owners * capacity
    score_scale = head_dim ** (-0.5)
    weight_piece = lax.all_gather(proj_weight, ("ctx", "clu"), axis=0, tiled=True)
    flat_piece = weight_piece.reshape(weight_piece.shape[0], 2 * proj_width)
    summed = jnp.dot(local_rows, flat_piece, preferred_element_type=jnp.float32)
    projected = summed.astype(jnp.bfloat16)
    queries = projected[:, :proj_width].reshape(row_count, heads_here, head_dim)
    values = projected[:, proj_width:].reshape(row_count, heads_here, head_dim)
    features = jnp.concatenate([queries, values], axis=2).transpose(1, 0, 2)
    cluster_ids = clusters[0]
    owner_of = cluster_ids // per_owner
    onehot = (owner_of[:, :, None] == jnp.arange(owners, dtype=jnp.int32)[None, None, :]).astype(
        jnp.int32
    )
    rank_in = jnp.sum((jnp.cumsum(onehot, axis=0) - onehot) * onehot, axis=2)
    slot_of = (owner_of * capacity + rank_in).T
    head_rows = jnp.arange(heads_here, dtype=jnp.int32)[:, None]
    token_index = jnp.broadcast_to(
        jnp.arange(row_count, dtype=jnp.int32)[None, :], (heads_here, row_count)
    )
    source = jnp.zeros((heads_here, total_slots), jnp.int32).at[head_rows, slot_of].set(token_index)
    positions = lax.axis_index("clu") * row_count + jnp.arange(row_count, dtype=jnp.int32)
    labels = cluster_ids.T * length + positions[None, :]
    slot_tags = (
        jnp.full((heads_here, total_slots), -1, jnp.int32).at[head_rows, slot_of].set(labels)
    )
    outgoing = jnp.take_along_axis(features, source[:, :, None], axis=1)
    outgoing = jnp.where((slot_tags >= 0)[:, :, None], outgoing, jnp.zeros_like(outgoing))
    outgoing = outgoing.reshape(heads_here, owners, capacity, 2 * head_dim)
    slot_tags = slot_tags.reshape(heads_here, owners, capacity)

    def attend_head(head_item):
        slot_block, key_tags = head_item
        flattened = slot_block.reshape(-1, 2 * head_dim)
        key_rows = flattened[:, :head_dim]
        value_rows = flattened[:, head_dim:]
        key_tags = key_tags.reshape(-1)
        scores = (
            jnp.einsum("qd,kd->qk", key_rows, key_rows, preferred_element_type=jnp.float32)
            * score_scale
        )
        tag_group = key_tags // length
        tag_pos = key_tags % length
        admitted = (
            (key_tags[None, :] >= 0)
            & (tag_group[None, :] == tag_group[:, None])
            & (tag_pos[None, :] <= tag_pos[:, None])
        )
        scores = jnp.where(key_tags[None, :] == key_tags[:, None], -100000.0, scores)
        scores = jnp.where(admitted, scores, -1e30)
        row_max = jnp.max(scores, axis=1, keepdims=True)
        exp_scores = jnp.exp(scores - row_max)
        row_total = jnp.sum(exp_scores, axis=1, keepdims=True)
        probabilities = (exp_scores / row_total).astype(jnp.bfloat16)
        result = jnp.dot(probabilities, value_rows, preferred_element_type=jnp.float32).astype(
            jnp.bfloat16
        )
        return result.reshape(slot_block.shape[0], slot_block.shape[1], head_dim)

    replies = lax.map(
        attend_head,
        (
            lax.all_to_all(outgoing, "clu", split_axis=1, concat_axis=1, tiled=True),
            lax.all_to_all(slot_tags, "clu", split_axis=1, concat_axis=1, tiled=True),
        ),
    )
    returned = lax.all_to_all(replies, "clu", split_axis=1, concat_axis=1, tiled=True)
    returned = returned.reshape(heads_here, total_slots, head_dim)
    gathered = jnp.take_along_axis(returned, slot_of[:, :, None], axis=1)
    return gathered.transpose(1, 0, 2).reshape(1, row_count, heads_here * head_dim)


def solution(mesh):
    sizes = dict(mesh.shape)
    heads_here = 16 // sizes["tp"]
    by_head = sizes["ctx"] == 2 and sizes["tp"] == 4 and sizes["clu"] == heads_here == 4
    return jax.shard_map(
        head_body if by_head else body,
        mesh=mesh,
        in_specs=(P("ctx", "clu", None), P(("ctx", "clu"), None, "tp"), P("ctx", "clu", "tp")),
        out_specs=P("ctx", "clu", "tp"),
        check_vma=False,
    )
```

```python
import functools

import jax
import jax.numpy as jnp
from jax import lax
from jax.experimental import pallas as pl
from jax.experimental.pallas import tpu as pltpu
from jax.sharding import PartitionSpec as P

CLUSTERS = 64
LOG2E = 1.4426950408889634
MESH = pl.DeviceIdType.MESH


def head_kernel(
    owners, depth, head_dim, score_scale,
    tok_ref, w_ref, cl_ref, out_ref,
    rows, weights, stage, marks, ids, mine, part, theirs, proj, reply,
    own_sem, wm_send, wm_recv, wx_send, wx_recv, id_send, id_recv,
    cross_send, cross_recv, fwd_send, fwd_recv, mate_send, mate_recv,
    core_send, core_recv, y_send, y_recv, far_send, far_recv,
    part_send, part_recv, out_send, out_recv,
):
    a = lax.axis_index("ctx")
    c = lax.axis_index("clu")
    t = lax.axis_index("tp")
    k = lax.rem(t, 2)
    y = t // 2
    pair = c // 2
    side = lax.rem(c, 2)
    near = side != pair
    count = tok_ref.shape[0]
    short = count // 2
    cut = depth // 2
    half = tok_ref.shape[1] // 2
    run = half // 2
    quarter = half // 4
    core_peer = {"tp": y * 2 + 1 - k}
    y_peer = {"tp": (1 - y) * 2 + k}
    x_peer = {"ctx": 1 - a}
    mate = pair * 2 + 1 - side
    twin = (1 - pair) * 2 + side

    def at_clu(index):
        return {"clu": index}

    def remote(src, dst, send, recv, peer):
        return pltpu.make_async_remote_copy(
            src_ref=src, dst_ref=dst, send_sem=send, recv_sem=recv,
            device_id=peer, device_id_type=MESH,
        )

    def held(which, q):
        start = (q // 2) * half + which * run + lax.rem(q, 2) * quarter
        return pl.ds(pl.multiple_of(start, quarter), quarter)

    heads = (1 - pair, pair)

    def piece(ctx, at, role, e):
        start = pl.multiple_of((ctx * 2 + at) * depth + e * cut, cut)
        return weights.at[heads[role], pl.ds(start, cut)]

    barrier = pltpu.get_barrier_semaphore()
    others = [at_clu(lax.rem(c + d, owners)) for d in range(1, owners)]
    others += [core_peer, y_peer, x_peer]
    for peer in others:
        pl.semaphore_signal(barrier, inc=1, device_id=peer, device_id_type=MESH)
    local = [
        pltpu.make_async_copy(
            tok_ref.at[pl.ds(h * short, short), held(pair, q)], rows.at[c, h, q], own_sem.at[h * 4 + q]
        )
        for q in range(4) for h in range(2)
    ]
    for copy in local:
        copy.start()
    for head in range(owners):
        marks[head] = jnp.broadcast_to(cl_ref[head : head + 1, :], marks.shape[1:])
    ids[c] = marks[c]
    for role in range(2):
        for kind in range(2):
            lands = pl.ds(kind * head_dim, head_dim)
            start = pl.multiple_of((heads[role] * 2 + side) * head_dim, head_dim)
            mine_at = pl.ds(pl.multiple_of((a * 2 + side) * depth, depth), depth)
            weights[heads[role], mine_at, lands] = w_ref[kind, :, pl.ds(start, head_dim)]
            start = pl.multiple_of((heads[role] * 2 + 1 - side) * head_dim, head_dim)
            stage[role, :, lands] = w_ref[kind, :, pl.ds(start, head_dim)]
    pl.semaphore_wait(barrier, len(others))

    blocks = [
        (1 - pair) * 2 + pair,
        (1 - pair) * 2 + 1 - pair,
        mate,
    ]

    def cross(h):
        turn = jnp.where(near, 0, 1)
        return remote(
            tok_ref.at[pl.ds(h * short, short), held(1 - pair, t)], rows.at[c, h, t],
            cross_send.at[h], cross_recv.at[turn, h], at_clu(2 - pair),
        )

    def cross_came(n, h):
        here = rows.at[blocks[n], h, t]
        return remote(here, here, cross_send.at[h], cross_recv.at[n, h], at_clu(mate))

    def forward(n, h):
        here = rows.at[blocks[n], h, t]
        return remote(here, here, fwd_send.at[n, h], fwd_recv.at[n, h], at_clu(mate))

    def to_mate(h):
        return remote(
            tok_ref.at[pl.ds(h * short, short), held(pair, t)], rows.at[c, h, t],
            mate_send.at[h], mate_recv.at[h], at_clu(mate),
        )

    def mate_came(h):
        here = rows.at[mate, h, t]
        return remote(here, here, mate_send.at[h], mate_recv.at[h], at_clu(mate))

    def shared(n, h, q, send, recv, peer):
        here = rows.at[blocks[n], h, q]
        return remote(here, here, send.at[n, h], recv.at[n, h], peer)

    def to_core(n, h, q):
        return shared(n, h, q, core_send, core_recv, core_peer)

    def to_y(n, h, q):
        return shared(n, h, q, y_send, y_recv, y_peer)

    def to_core_far(n, h, q):
        return shared(n, h, q, far_send, far_recv, core_peer)

    def w_mate(role, e):
        return remote(
            stage.at[role, pl.ds(e * cut, cut)], piece(a, side, role, e),
            wm_send.at[role, e], wm_recv.at[role, e], at_clu(mate),
        )

    def w_mate_came(role, e):
        here = piece(a, 1 - side, role, e)
        return remote(here, here, wm_send.at[role, e], wm_recv.at[role, e], at_clu(mate))

    def w_cross(i, ctx, role, e):
        here = piece(ctx, side if i == 0 else 1 - side, role, e)
        return remote(here, here, wx_send.at[i, role, e], wx_recv.at[i, role, e], x_peer)

    def w_pass(role):
        for e in range(2):
            w_mate_came(role, e).wait_recv()
            w_cross(1, a, role, e).start()

    def w_ready(role):
        for i in range(2):
            for e in range(2):
                w_cross(i, 1 - a, role, e).wait_recv()

    def id_hop(d):
        goal = lax.rem(c + d, owners)
        return remote(marks.at[goal], ids.at[c], id_send.at[d - 1], id_recv.at[d - 1], at_clu(goal))

    def id_came(d):
        source = lax.rem(c + owners - d, owners)
        return remote(ids.at[source], ids.at[source], id_send.at[d - 1], id_recv.at[d - 1], at_clu(source))

    def part_hop(block, h):
        return remote(
            part.at[block, h], theirs.at[block, h],
            part_send.at[block, h], part_recv.at[block, h], at_clu(twin),
        )

    for h in range(2):
        cross(h).start()
    for role in range(2):
        for e in range(2):
            w_cross(0, a, role, e).start()
            if role == 0:
                w_mate(role, e).start()
        if role == 0:
            for h in range(2):
                to_mate(h).start()
    for d in range(1, owners):
        id_hop(d).start()

    def share(n, h):
        to_y(n, h, t).start()
        to_core(n, h, t).start()

    def relay(n):
        q = (1 - y) * 2 + k
        for h in range(2):
            to_y(n, h, q).wait_recv()
            to_core_far(n, h, q).start()

    def arrive_near(n):
        for h in range(2):
            cross_came(n, h).wait_recv()
            forward(n, h).start()
            share(n, h)

    def arrive_far(n):
        for h in range(2):
            forward(n, h).wait_recv()
            share(n, h)

    def whole(block, h):
        return jnp.concatenate([rows[block, h, q] for q in range(4)], axis=1)

    def give(block, h):
        given = jnp.dot(whole(block, h), weights[1 - pair], preferred_element_type=jnp.float32)
        part[block, h] = given.astype(jnp.bfloat16)
        part_hop(block, h).start()

    def finish(n):
        for h in range(2):
            to_core(n, h, y * 2 + 1 - k).wait_recv()
            to_core_far(n, h, (1 - y) * 2 + 1 - k).wait_recv()
            give(blocks[n], h)

    pl.when(near)(lambda: arrive_near(0))
    w_pass(0)
    pl.when(near)(lambda: arrive_near(1))
    for e in range(2):
        w_mate(1, e).start()
    for h in range(2):
        mate_came(h).wait_recv()
        share(2, h)
    pl.when(jnp.logical_not(near))(lambda: arrive_far(0))
    relay(2)
    for copy in local:
        copy.wait()
    w_ready(0)
    for h in range(2):
        give(c, h)
    finish(2)
    relay(0)
    finish(0)
    pl.when(jnp.logical_not(near))(lambda: arrive_far(1))
    w_pass(1)
    relay(1)
    finish(1)
    w_ready(1)
    for block in range(owners):
        both = jnp.concatenate([whole(block, h) for h in range(2)], axis=0)
        mine[block] = jnp.dot(both, weights[pair], preferred_element_type=jnp.float32)
    for d in range(1, owners):
        id_came(d).wait_recv()
    for block in range(owners):
        for h in range(2):
            part_hop(block, h).wait_recv()
            proj[block, h * short : (h + 1) * short] = (
                mine[block, h * short : (h + 1) * short] + theirs[block, h].astype(jnp.float32)
            ).astype(jnp.bfloat16)

    def send_reply(goal):
        return remote(
            reply.at[goal], out_ref.at[:, pl.ds(pl.multiple_of(c * head_dim, head_dim), head_dim)],
            out_send.at[goal], out_recv.at[c], at_clu(goal),
        )

    def keep_reply(goal):
        return pltpu.make_async_copy(
            reply.at[goal], out_ref.at[:, pl.ds(pl.multiple_of(c * head_dim, head_dim), head_dim)],
            out_send.at[goal],
        )

    for goal in reversed(range(owners)):
        query = proj[goal, :, :head_dim]
        query_ids = jnp.transpose(ids[goal])[:, :1]
        parts = []
        for block in range(goal + 1):
            scores = lax.dot_general(
                query, proj[block, :, :head_dim], (((1,), (1,)), ((), ())),
                preferred_element_type=jnp.float32,
            ) * (score_scale * LOG2E)
            admitted = query_ids == ids[block, :1, :]
            if block == goal:
                at = lax.broadcasted_iota(jnp.int32, (count, count), 0)
                to = lax.broadcasted_iota(jnp.int32, (count, count), 1)
                scores = jnp.where(at == to, -100000.0 * LOG2E, scores)
                admitted = admitted & (to <= at)
            parts.append(jnp.where(admitted, scores, -1e30))
        top = functools.reduce(jnp.maximum, [jnp.max(p, axis=1, keepdims=True) for p in parts])
        total = jnp.zeros((count, 1), jnp.float32)
        mixed = jnp.zeros((count, head_dim), jnp.float32)
        for block, piece_scores in enumerate(parts):
            weighed = jnp.exp2(piece_scores - top)
            total += jnp.sum(weighed, axis=1, keepdims=True)
            mixed += jnp.dot(
                weighed.astype(jnp.bfloat16), proj[block, :, head_dim:],
                preferred_element_type=jnp.float32,
            )
        reply[goal] = (mixed / total).astype(jnp.bfloat16)
        pl.when(c != goal)(lambda goal=goal: send_reply(goal).start())
        pl.when(c == goal)(lambda goal=goal: keep_reply(goal).start())

    for h in range(2):
        cross(h).wait_send()
        to_mate(h).wait_send()
        for n in range(2):
            pl.when(near)(lambda n=n, h=h: forward(n, h).wait_send())
        for n in range(3):
            to_y(n, h, t).wait_send()
            to_core(n, h, t).wait_send()
            to_core_far(n, h, (1 - y) * 2 + k).wait_send()
        for block in range(owners):
            part_hop(block, h).wait_send()
    for role in range(2):
        for e in range(2):
            w_mate(role, e).wait_send()
            for i in range(2):
                w_cross(i, a, role, e).wait_send()
    for d in range(1, owners):
        id_hop(d).wait_send()
    for goal in range(owners):
        @pl.when(c != goal)
        def _(goal=goal):
            send_reply(goal).wait_send()
            column = out_ref.at[:, pl.ds(goal * head_dim, head_dim)]
            remote(reply.at[goal], column, out_send.at[goal], out_recv.at[goal], at_clu(goal)).wait_recv()

        pl.when(c == goal)(lambda goal=goal: keep_reply(goal).wait())


def head_body(tokens, proj_weight, clusters):
    row_count, width = tokens.shape[1:]
    owners = lax.axis_size("clu")
    heads_here = clusters.shape[2]
    depth, _, proj_width = proj_weight.shape
    head_dim = proj_width // heads_here
    kinds = proj_weight.transpose(1, 0, 2)
    steps = owners - 1
    dma = pltpu.SemaphoreType.DMA
    split = (owners, 2, row_count // 2, 2 * head_dim)
    out = pl.pallas_call(
        functools.partial(head_kernel, owners, depth, head_dim, head_dim ** (-0.5)),
        out_shape=jax.ShapeDtypeStruct((row_count, proj_width), jnp.bfloat16),
        in_specs=[pl.BlockSpec(memory_space=space) for space in (pl.ANY, pltpu.VMEM, pltpu.VMEM)],
        out_specs=pl.BlockSpec(memory_space=pl.ANY),
        scratch_shapes=[
            pltpu.VMEM((owners, 2, 4, row_count // 2, width // 8), jnp.bfloat16),
            pltpu.VMEM((2, width // 2, 2 * head_dim), jnp.bfloat16),
            pltpu.VMEM((2, depth, 2 * head_dim), jnp.bfloat16),
            pltpu.VMEM((owners, 8, row_count), jnp.int32),
            pltpu.VMEM((owners, 8, row_count), jnp.int32),
            pltpu.VMEM((owners, row_count, 2 * head_dim), jnp.float32),
            pltpu.VMEM(split, jnp.bfloat16),
            pltpu.VMEM(split, jnp.bfloat16),
            pltpu.VMEM((owners, row_count, 2 * head_dim), jnp.bfloat16),
            pltpu.VMEM((owners, row_count, head_dim), jnp.bfloat16),
            dma((8,)),
            dma((2, 2)), dma((2, 2)),
            dma((2, 2, 2)), dma((2, 2, 2)),
            dma((steps,)), dma((steps,)),
            dma((2,)), dma((2, 2)),
            dma((2, 2)), dma((2, 2)),
            dma((2,)), dma((2,)),
            dma((3, 2)), dma((3, 2)),
            dma((3, 2)), dma((3, 2)),
            dma((3, 2)), dma((3, 2)),
            dma((owners, 2)), dma((owners, 2)),
            dma((owners,)), dma((owners,)),
        ],
        compiler_params=pltpu.CompilerParams(
            collective_id=0, has_side_effects=True, vmem_limit_bytes=40 * 1024 * 1024
        ),
    )(tokens[0], kinds, clusters[0].T)
    return out[None]


def body(tokens, proj_weight, clusters):
    local_rows = tokens[0]
    row_count = local_rows.shape[0]
    owners = lax.axis_size("clu")
    heads_here = clusters.shape[2]
    proj_width = proj_weight.shape[2]
    head_dim = proj_width // heads_here
    capacity = 2 * row_count // owners
    per_owner = CLUSTERS // owners
    length = row_count * owners
    total_slots = owners * capacity
    score_scale = head_dim ** (-0.5)
    weight_piece = lax.all_gather(proj_weight, ("ctx", "clu"), axis=0, tiled=True)
    flat_piece = weight_piece.reshape(weight_piece.shape[0], 2 * proj_width)
    summed = jnp.dot(local_rows, flat_piece, preferred_element_type=jnp.float32)
    projected = summed.astype(jnp.bfloat16)
    queries = projected[:, :proj_width].reshape(row_count, heads_here, head_dim)
    values = projected[:, proj_width:].reshape(row_count, heads_here, head_dim)
    features = jnp.concatenate([queries, values], axis=2).transpose(1, 0, 2)
    cluster_ids = clusters[0]
    owner_of = cluster_ids // per_owner
    onehot = (owner_of[:, :, None] == jnp.arange(owners, dtype=jnp.int32)[None, None, :]).astype(
        jnp.int32
    )
    rank_in = jnp.sum((jnp.cumsum(onehot, axis=0) - onehot) * onehot, axis=2)
    slot_of = (owner_of * capacity + rank_in).T
    head_rows = jnp.arange(heads_here, dtype=jnp.int32)[:, None]
    token_index = jnp.broadcast_to(
        jnp.arange(row_count, dtype=jnp.int32)[None, :], (heads_here, row_count)
    )
    source = jnp.zeros((heads_here, total_slots), jnp.int32).at[head_rows, slot_of].set(token_index)
    positions = lax.axis_index("clu") * row_count + jnp.arange(row_count, dtype=jnp.int32)
    labels = cluster_ids.T * length + positions[None, :]
    slot_tags = (
        jnp.full((heads_here, total_slots), -1, jnp.int32).at[head_rows, slot_of].set(labels)
    )
    outgoing = jnp.take_along_axis(features, source[:, :, None], axis=1)
    outgoing = jnp.where((slot_tags >= 0)[:, :, None], outgoing, jnp.zeros_like(outgoing))
    outgoing = outgoing.reshape(heads_here, owners, capacity, 2 * head_dim)
    slot_tags = slot_tags.reshape(heads_here, owners, capacity)

    def attend_head(head_item):
        slot_block, key_tags = head_item
        flattened = slot_block.reshape(-1, 2 * head_dim)
        key_rows = flattened[:, :head_dim]
        value_rows = flattened[:, head_dim:]
        key_tags = key_tags.reshape(-1)
        scores = (
            jnp.einsum("qd,kd->qk", key_rows, key_rows, preferred_element_type=jnp.float32)
            * score_scale
        )
        tag_group = key_tags // length
        tag_pos = key_tags % length
        admitted = (
            (key_tags[None, :] >= 0)
            & (tag_group[None, :] == tag_group[:, None])
            & (tag_pos[None, :] <= tag_pos[:, None])
        )
        scores = jnp.where(key_tags[None, :] == key_tags[:, None], -100000.0, scores)
        scores = jnp.where(admitted, scores, -1e30)
        row_max = jnp.max(scores, axis=1, keepdims=True)
        exp_scores = jnp.exp(scores - row_max)
        row_total = jnp.sum(exp_scores, axis=1, keepdims=True)
        probabilities = (exp_scores / row_total).astype(jnp.bfloat16)
        result = jnp.dot(probabilities, value_rows, preferred_element_type=jnp.float32).astype(
            jnp.bfloat16
        )
        return result.reshape(slot_block.shape[0], slot_block.shape[1], head_dim)

    replies = lax.map(
        attend_head,
        (
            lax.all_to_all(outgoing, "clu", split_axis=1, concat_axis=1, tiled=True),
            lax.all_to_all(slot_tags, "clu", split_axis=1, concat_axis=1, tiled=True),
        ),
    )
    returned = lax.all_to_all(replies, "clu", split_axis=1, concat_axis=1, tiled=True)
    returned = returned.reshape(heads_here, total_slots, head_dim)
    gathered = jnp.take_along_axis(returned, slot_of[:, :, None], axis=1)
    return gathered.transpose(1, 0, 2).reshape(1, row_count, heads_here * head_dim)


def solution(mesh):
    sizes = dict(mesh.shape)
    heads_here = 16 // sizes["tp"]
    by_head = sizes["ctx"] == 2 and sizes["tp"] == 4 and sizes["clu"] == heads_here == 4
    return jax.shard_map(
        head_body if by_head else body,
        mesh=mesh,
        in_specs=(P("ctx", "clu", None), P(("ctx", "clu"), None, "tp"), P("ctx", "clu", "tp")),
        out_specs=P("ctx", "clu", "tp"),
        check_vma=False,
    )
```

```python
import functools

import jax
import jax.numpy as jnp
from jax import lax
from jax.experimental import pallas as pl
from jax.experimental.pallas import tpu as pltpu
from jax.sharding import PartitionSpec as P

CLUSTERS = 64
LOG2E = 1.4426950408889634
MESH = pl.DeviceIdType.MESH


def head_kernel(
    owners, depth, head_dim, score_scale,
    tok_ref, w_ref, cl_ref, out_ref,
    rows, weights, stage, marks, ids, mine, part, theirs, proj, reply,
    own_sem, wm_send, wm_recv, wx_send, wx_recv, id_send, id_recv,
    cross_send, cross_recv, fwd_send, fwd_recv, mate_send, mate_recv,
    core_send, core_recv, y_send, y_recv, far_send, far_recv,
    part_send, part_recv, out_send, out_recv,
):
    a = lax.axis_index("ctx")
    c = lax.axis_index("clu")
    t = lax.axis_index("tp")
    k = lax.rem(t, 2)
    y = t // 2
    pair = c // 2
    side = lax.rem(c, 2)
    near = side != pair
    count = tok_ref.shape[0]
    short = count // 2
    cut = depth // 2
    half = tok_ref.shape[1] // 2
    run = half // 2
    quarter = half // 4
    core_peer = {"tp": y * 2 + 1 - k}
    y_peer = {"tp": (1 - y) * 2 + k}
    x_peer = {"ctx": 1 - a}
    mate = pair * 2 + 1 - side
    twin = (1 - pair) * 2 + side

    def at_clu(index):
        return {"clu": index}

    def remote(src, dst, send, recv, peer):
        return pltpu.make_async_remote_copy(
            src_ref=src, dst_ref=dst, send_sem=send, recv_sem=recv,
            device_id=peer, device_id_type=MESH,
        )

    def held(which, q):
        start = (q // 2) * half + which * run + lax.rem(q, 2) * quarter
        return pl.ds(pl.multiple_of(start, quarter), quarter)

    heads = (1 - pair, pair)

    def piece(ctx, at, role, e):
        start = pl.multiple_of((ctx * 2 + at) * depth + e * cut, cut)
        return weights.at[heads[role], pl.ds(start, cut)]

    barrier = pltpu.get_barrier_semaphore()
    others = [at_clu(lax.rem(c + d, owners)) for d in range(1, owners)]
    others += [core_peer, y_peer, x_peer]
    for peer in others:
        pl.semaphore_signal(barrier, inc=1, device_id=peer, device_id_type=MESH)
    local = [
        pltpu.make_async_copy(
            tok_ref.at[pl.ds(h * short, short), held(pair, q)], rows.at[c, h, q], own_sem.at[h * 4 + q]
        )
        for q in range(4) for h in range(2)
    ]
    for copy in local:
        copy.start()
    for head in range(owners):
        marks[head] = jnp.broadcast_to(cl_ref[head : head + 1, :], marks.shape[1:])
    ids[c] = marks[c]
    for role in range(2):
        for kind in range(2):
            lands = pl.ds(kind * head_dim, head_dim)
            start = pl.multiple_of((heads[role] * 2 + side) * head_dim, head_dim)
            mine_at = pl.ds(pl.multiple_of((a * 2 + side) * depth, depth), depth)
            weights[heads[role], mine_at, lands] = w_ref[kind, :, pl.ds(start, head_dim)]
            start = pl.multiple_of((heads[role] * 2 + 1 - side) * head_dim, head_dim)
            stage[role, :, lands] = w_ref[kind, :, pl.ds(start, head_dim)]
    pl.semaphore_wait(barrier, len(others))

    blocks = [
        (1 - pair) * 2 + pair,
        (1 - pair) * 2 + 1 - pair,
        mate,
    ]

    def cross(h):
        turn = jnp.where(near, 0, 1)
        return remote(
            tok_ref.at[pl.ds(h * short, short), held(1 - pair, t)], rows.at[c, h, t],
            cross_send.at[h], cross_recv.at[turn, h], at_clu(2 - pair),
        )

    def cross_came(n, h):
        here = rows.at[blocks[n], h, t]
        return remote(here, here, cross_send.at[h], cross_recv.at[n, h], at_clu(mate))

    def forward(n, h):
        here = rows.at[blocks[n], h, t]
        return remote(here, here, fwd_send.at[n, h], fwd_recv.at[n, h], at_clu(mate))

    def to_mate(h):
        return remote(
            tok_ref.at[pl.ds(h * short, short), held(pair, t)], rows.at[c, h, t],
            mate_send.at[h], mate_recv.at[h], at_clu(mate),
        )

    def mate_came(h):
        here = rows.at[mate, h, t]
        return remote(here, here, mate_send.at[h], mate_recv.at[h], at_clu(mate))

    def shared(n, h, q, send, recv, peer):
        here = rows.at[blocks[n], h, q]
        return remote(here, here, send.at[n, h], recv.at[n, h], peer)

    def to_core(n, h, q):
        return shared(n, h, q, core_send, core_recv, core_peer)

    def to_y(n, h, q):
        return shared(n, h, q, y_send, y_recv, y_peer)

    def to_core_far(n, h, q):
        return shared(n, h, q, far_send, far_recv, core_peer)

    def w_mate(role, e):
        return remote(
            stage.at[role, pl.ds(e * cut, cut)], piece(a, side, role, e),
            wm_send.at[role, e], wm_recv.at[role, e], at_clu(mate),
        )

    def w_mate_came(role, e):
        here = piece(a, 1 - side, role, e)
        return remote(here, here, wm_send.at[role, e], wm_recv.at[role, e], at_clu(mate))

    def w_cross(i, ctx, role, e):
        here = piece(ctx, side if i == 0 else 1 - side, role, e)
        return remote(here, here, wx_send.at[i, role, e], wx_recv.at[i, role, e], x_peer)

    def w_pass(role):
        for e in range(2):
            w_mate_came(role, e).wait_recv()
            w_cross(1, a, role, e).start()

    def w_ready(role):
        for i in range(2):
            for e in range(2):
                w_cross(i, 1 - a, role, e).wait_recv()

    def id_hop(d):
        goal = lax.rem(c + d, owners)
        return remote(marks.at[goal], ids.at[c], id_send.at[d - 1], id_recv.at[d - 1], at_clu(goal))

    def id_came(d):
        source = lax.rem(c + owners - d, owners)
        return remote(ids.at[source], ids.at[source], id_send.at[d - 1], id_recv.at[d - 1], at_clu(source))

    def part_hop(block, h):
        return remote(
            part.at[block, h], theirs.at[block, h],
            part_send.at[block, h], part_recv.at[block, h], at_clu(twin),
        )

    for h in range(2):
        cross(h).start()
    for role in range(2):
        for e in range(2):
            w_cross(0, a, role, e).start()
            if role == 0:
                w_mate(role, e).start()
        if role == 0:
            for h in range(2):
                to_mate(h).start()
    for d in range(1, owners):
        id_hop(d).start()

    def share(n, h):
        to_y(n, h, t).start()
        to_core(n, h, t).start()

    def relay(n):
        q = (1 - y) * 2 + k
        for h in range(2):
            to_y(n, h, q).wait_recv()
            to_core_far(n, h, q).start()

    def arrive_near(n):
        for h in range(2):
            cross_came(n, h).wait_recv()
            forward(n, h).start()
            share(n, h)

    def arrive_far(n):
        for h in range(2):
            forward(n, h).wait_recv()
            share(n, h)

    def whole(block, h):
        return jnp.concatenate([rows[block, h, q] for q in range(4)], axis=1)

    def give(block, h):
        given = jnp.dot(whole(block, h), weights[1 - pair], preferred_element_type=jnp.float32)
        part[block, h] = given.astype(jnp.bfloat16)
        part_hop(block, h).start()

    def finish(n):
        for h in range(2):
            to_core(n, h, y * 2 + 1 - k).wait_recv()
            to_core_far(n, h, (1 - y) * 2 + 1 - k).wait_recv()
            give(blocks[n], h)

    pl.when(near)(lambda: arrive_near(0))
    w_pass(0)
    pl.when(near)(lambda: arrive_near(1))
    for e in range(2):
        w_mate(1, e).start()
    for h in range(2):
        mate_came(h).wait_recv()
        share(2, h)
    pl.when(jnp.logical_not(near))(lambda: arrive_far(0))
    relay(2)
    for copy in local:
        copy.wait()
    w_ready(0)
    for h in range(2):
        give(c, h)
    finish(2)
    relay(0)
    finish(0)
    pl.when(jnp.logical_not(near))(lambda: arrive_far(1))
    w_pass(1)
    relay(1)
    finish(1)
    w_ready(1)
    for block in range(owners):
        both = jnp.concatenate([whole(block, h) for h in range(2)], axis=0)
        mine[block] = jnp.dot(both, weights[pair], preferred_element_type=jnp.float32)
    for d in range(1, owners):
        id_came(d).wait_recv()
    for block in range(owners):
        for h in range(2):
            part_hop(block, h).wait_recv()
            proj[block, h * short : (h + 1) * short] = (
                mine[block, h * short : (h + 1) * short] + theirs[block, h].astype(jnp.float32)
            ).astype(jnp.bfloat16)

    def send_reply(goal):
        return remote(
            reply.at[goal], out_ref.at[:, pl.ds(pl.multiple_of(c * head_dim, head_dim), head_dim)],
            out_send.at[goal], out_recv.at[c], at_clu(goal),
        )

    def keep_reply(goal):
        return pltpu.make_async_copy(
            reply.at[goal], out_ref.at[:, pl.ds(pl.multiple_of(c * head_dim, head_dim), head_dim)],
            out_send.at[goal],
        )

    for goal in reversed(range(owners)):
        query = proj[goal, :, :head_dim]
        query_ids = jnp.transpose(ids[goal])[:, :1]
        parts = []
        for block in range(goal + 1):
            scores = lax.dot_general(
                query, proj[block, :, :head_dim], (((1,), (1,)), ((), ())),
                preferred_element_type=jnp.float32,
            ) * (score_scale * LOG2E)
            admitted = query_ids == ids[block, :1, :]
            if block == goal:
                at = lax.broadcasted_iota(jnp.int32, (count, count), 0)
                to = lax.broadcasted_iota(jnp.int32, (count, count), 1)
                scores = jnp.where(at == to, -100000.0 * LOG2E, scores)
                admitted = admitted & (to <= at)
            parts.append(jnp.where(admitted, scores, -1e30))
        top = jnp.max(functools.reduce(jnp.maximum, parts), axis=1, keepdims=True)
        mixed = jnp.zeros((count, 2 * head_dim), jnp.float32)
        for block, piece_scores in enumerate(parts):
            weighed = jnp.exp2(piece_scores - top).astype(jnp.bfloat16)
            summands = jnp.concatenate(
                [proj[block, :, head_dim:], jnp.ones((count, head_dim), jnp.bfloat16)], axis=1
            )
            mixed += jnp.dot(weighed, summands, preferred_element_type=jnp.float32)
        reply[goal] = (mixed[:, :head_dim] / mixed[:, head_dim:]).astype(jnp.bfloat16)
        pl.when(c != goal)(lambda goal=goal: send_reply(goal).start())
        pl.when(c == goal)(lambda goal=goal: keep_reply(goal).start())

    for h in range(2):
        cross(h).wait_send()
        to_mate(h).wait_send()
        for n in range(2):
            pl.when(near)(lambda n=n, h=h: forward(n, h).wait_send())
        for n in range(3):
            to_y(n, h, t).wait_send()
            to_core(n, h, t).wait_send()
            to_core_far(n, h, (1 - y) * 2 + k).wait_send()
        for block in range(owners):
            part_hop(block, h).wait_send()
    for role in range(2):
        for e in range(2):
            w_mate(role, e).wait_send()
            for i in range(2):
                w_cross(i, a, role, e).wait_send()
    for d in range(1, owners):
        id_hop(d).wait_send()
    for goal in range(owners):
        @pl.when(c != goal)
        def _(goal=goal):
            send_reply(goal).wait_send()
            column = out_ref.at[:, pl.ds(goal * head_dim, head_dim)]
            remote(reply.at[goal], column, out_send.at[goal], out_recv.at[goal], at_clu(goal)).wait_recv()

        pl.when(c == goal)(lambda goal=goal: keep_reply(goal).wait())


def head_body(tokens, proj_weight, clusters):
    row_count, width = tokens.shape[1:]
    owners = lax.axis_size("clu")
    heads_here = clusters.shape[2]
    depth, _, proj_width = proj_weight.shape
    head_dim = proj_width // heads_here
    kinds = proj_weight.transpose(1, 0, 2)
    steps = owners - 1
    dma = pltpu.SemaphoreType.DMA
    split = (owners, 2, row_count // 2, 2 * head_dim)
    out = pl.pallas_call(
        functools.partial(head_kernel, owners, depth, head_dim, head_dim ** (-0.5)),
        out_shape=jax.ShapeDtypeStruct((row_count, proj_width), jnp.bfloat16),
        in_specs=[pl.BlockSpec(memory_space=space) for space in (pl.ANY, pltpu.VMEM, pltpu.VMEM)],
        out_specs=pl.BlockSpec(memory_space=pl.ANY),
        scratch_shapes=[
            pltpu.VMEM((owners, 2, 4, row_count // 2, width // 8), jnp.bfloat16),
            pltpu.VMEM((2, width // 2, 2 * head_dim), jnp.bfloat16),
            pltpu.VMEM((2, depth, 2 * head_dim), jnp.bfloat16),
            pltpu.VMEM((owners, 8, row_count), jnp.int32),
            pltpu.VMEM((owners, 8, row_count), jnp.int32),
            pltpu.VMEM((owners, row_count, 2 * head_dim), jnp.float32),
            pltpu.VMEM(split, jnp.bfloat16),
            pltpu.VMEM(split, jnp.bfloat16),
            pltpu.VMEM((owners, row_count, 2 * head_dim), jnp.bfloat16),
            pltpu.VMEM((owners, row_count, head_dim), jnp.bfloat16),
            dma((8,)),
            dma((2, 2)), dma((2, 2)),
            dma((2, 2, 2)), dma((2, 2, 2)),
            dma((steps,)), dma((steps,)),
            dma((2,)), dma((2, 2)),
            dma((2, 2)), dma((2, 2)),
            dma((2,)), dma((2,)),
            dma((3, 2)), dma((3, 2)),
            dma((3, 2)), dma((3, 2)),
            dma((3, 2)), dma((3, 2)),
            dma((owners, 2)), dma((owners, 2)),
            dma((owners,)), dma((owners,)),
        ],
        compiler_params=pltpu.CompilerParams(
            collective_id=0, has_side_effects=True, vmem_limit_bytes=40 * 1024 * 1024
        ),
    )(tokens[0], kinds, clusters[0].T)
    return out[None]


def body(tokens, proj_weight, clusters):
    local_rows = tokens[0]
    row_count = local_rows.shape[0]
    owners = lax.axis_size("clu")
    heads_here = clusters.shape[2]
    proj_width = proj_weight.shape[2]
    head_dim = proj_width // heads_here
    capacity = 2 * row_count // owners
    per_owner = CLUSTERS // owners
    length = row_count * owners
    total_slots = owners * capacity
    score_scale = head_dim ** (-0.5)
    weight_piece = lax.all_gather(proj_weight, ("ctx", "clu"), axis=0, tiled=True)
    flat_piece = weight_piece.reshape(weight_piece.shape[0], 2 * proj_width)
    summed = jnp.dot(local_rows, flat_piece, preferred_element_type=jnp.float32)
    projected = summed.astype(jnp.bfloat16)
    queries = projected[:, :proj_width].reshape(row_count, heads_here, head_dim)
    values = projected[:, proj_width:].reshape(row_count, heads_here, head_dim)
    features = jnp.concatenate([queries, values], axis=2).transpose(1, 0, 2)
    cluster_ids = clusters[0]
    owner_of = cluster_ids // per_owner
    onehot = (owner_of[:, :, None] == jnp.arange(owners, dtype=jnp.int32)[None, None, :]).astype(
        jnp.int32
    )
    rank_in = jnp.sum((jnp.cumsum(onehot, axis=0) - onehot) * onehot, axis=2)
    slot_of = (owner_of * capacity + rank_in).T
    head_rows = jnp.arange(heads_here, dtype=jnp.int32)[:, None]
    token_index = jnp.broadcast_to(
        jnp.arange(row_count, dtype=jnp.int32)[None, :], (heads_here, row_count)
    )
    source = jnp.zeros((heads_here, total_slots), jnp.int32).at[head_rows, slot_of].set(token_index)
    positions = lax.axis_index("clu") * row_count + jnp.arange(row_count, dtype=jnp.int32)
    labels = cluster_ids.T * length + positions[None, :]
    slot_tags = (
        jnp.full((heads_here, total_slots), -1, jnp.int32).at[head_rows, slot_of].set(labels)
    )
    outgoing = jnp.take_along_axis(features, source[:, :, None], axis=1)
    outgoing = jnp.where((slot_tags >= 0)[:, :, None], outgoing, jnp.zeros_like(outgoing))
    outgoing = outgoing.reshape(heads_here, owners, capacity, 2 * head_dim)
    slot_tags = slot_tags.reshape(heads_here, owners, capacity)

    def attend_head(head_item):
        slot_block, key_tags = head_item
        flattened = slot_block.reshape(-1, 2 * head_dim)
        key_rows = flattened[:, :head_dim]
        value_rows = flattened[:, head_dim:]
        key_tags = key_tags.reshape(-1)
        scores = (
            jnp.einsum("qd,kd->qk", key_rows, key_rows, preferred_element_type=jnp.float32)
            * score_scale
        )
        tag_group = key_tags // length
        tag_pos = key_tags % length
        admitted = (
            (key_tags[None, :] >= 0)
            & (tag_group[None, :] == tag_group[:, None])
            & (tag_pos[None, :] <= tag_pos[:, None])
        )
        scores = jnp.where(key_tags[None, :] == key_tags[:, None], -100000.0, scores)
        scores = jnp.where(admitted, scores, -1e30)
        row_max = jnp.max(scores, axis=1, keepdims=True)
        exp_scores = jnp.exp(scores - row_max)
        row_total = jnp.sum(exp_scores, axis=1, keepdims=True)
        probabilities = (exp_scores / row_total).astype(jnp.bfloat16)
        result = jnp.dot(probabilities, value_rows, preferred_element_type=jnp.float32).astype(
            jnp.bfloat16
        )
        return result.reshape(slot_block.shape[0], slot_block.shape[1], head_dim)

    replies = lax.map(
        attend_head,
        (
            lax.all_to_all(outgoing, "clu", split_axis=1, concat_axis=1, tiled=True),
            lax.all_to_all(slot_tags, "clu", split_axis=1, concat_axis=1, tiled=True),
        ),
    )
    returned = lax.all_to_all(replies, "clu", split_axis=1, concat_axis=1, tiled=True)
    returned = returned.reshape(heads_here, total_slots, head_dim)
    gathered = jnp.take_along_axis(returned, slot_of[:, :, None], axis=1)
    return gathered.transpose(1, 0, 2).reshape(1, row_count, heads_here * head_dim)


def solution(mesh):
    sizes = dict(mesh.shape)
    heads_here = 16 // sizes["tp"]
    by_head = sizes["ctx"] == 2 and sizes["tp"] == 4 and sizes["clu"] == heads_here == 4
    return jax.shard_map(
        head_body if by_head else body,
        mesh=mesh,
        in_specs=(P("ctx", "clu", None), P(("ctx", "clu"), None, "tp"), P("ctx", "clu", "tp")),
        out_specs=P("ctx", "clu", "tp"),
        check_vma=False,
    )
```

```python
import functools

import jax
import jax.numpy as jnp
from jax import lax
from jax.experimental import pallas as pl
from jax.experimental.pallas import tpu as pltpu
from jax.sharding import PartitionSpec as P

CLUSTERS = 64
LOG2E = 1.4426950408889634
MESH = pl.DeviceIdType.MESH


def head_kernel(
    owners, depth, head_dim, score_scale,
    tok_ref, w_ref, cl_ref, out_ref,
    rows, weights, stage, marks, ids, mine, part, theirs, proj, reply,
    own_sem, wm_send, wm_recv, wx_send, wx_recv, id_send, id_recv,
    cross_send, cross_recv, fwd_send, fwd_recv, mate_send, mate_recv,
    core_send, core_recv, y_send, y_recv, far_send, far_recv,
    part_send, part_recv, out_send, out_recv,
):
    a = lax.axis_index("ctx")
    c = lax.axis_index("clu")
    t = lax.axis_index("tp")
    k = lax.rem(t, 2)
    y = t // 2
    pair = c // 2
    side = lax.rem(c, 2)
    near = side != pair
    count = tok_ref.shape[0]
    short = count // 2
    cut = depth // 2
    half = tok_ref.shape[1] // 2
    run = half // 2
    quarter = half // 4
    core_peer = {"tp": y * 2 + 1 - k}
    y_peer = {"tp": (1 - y) * 2 + k}
    x_peer = {"ctx": 1 - a}
    mate = pair * 2 + 1 - side
    twin = (1 - pair) * 2 + side

    def at_clu(index):
        return {"clu": index}

    def remote(src, dst, send, recv, peer):
        return pltpu.make_async_remote_copy(
            src_ref=src, dst_ref=dst, send_sem=send, recv_sem=recv,
            device_id=peer, device_id_type=MESH,
        )

    def held(which, q):
        start = (q // 2) * half + which * run + lax.rem(q, 2) * quarter
        return pl.ds(pl.multiple_of(start, quarter), quarter)

    heads = (1 - pair, pair)

    def piece(ctx, at, role, e):
        start = pl.multiple_of((ctx * 2 + at) * depth + e * cut, cut)
        return weights.at[heads[role], pl.ds(start, cut)]

    barrier = pltpu.get_barrier_semaphore()
    others = [at_clu(lax.rem(c + d, owners)) for d in range(1, owners)]
    others += [core_peer, y_peer, x_peer]
    for peer in others:
        pl.semaphore_signal(barrier, inc=1, device_id=peer, device_id_type=MESH)
    local = [
        pltpu.make_async_copy(
            tok_ref.at[pl.ds(h * short, short), held(pair, q)], rows.at[c, h, q], own_sem.at[h * 4 + q]
        )
        for q in range(4) for h in range(2)
    ]
    for copy in local:
        copy.start()
    for head in range(owners):
        marks[head] = jnp.broadcast_to(cl_ref[head : head + 1, :], marks.shape[1:])
    ids[c] = marks[c]
    for role in range(2):
        for kind in range(2):
            lands = pl.ds(kind * head_dim, head_dim)
            start = pl.multiple_of((heads[role] * 2 + side) * head_dim, head_dim)
            mine_at = pl.ds(pl.multiple_of((a * 2 + side) * depth, depth), depth)
            weights[heads[role], mine_at, lands] = w_ref[kind, :, pl.ds(start, head_dim)]
            start = pl.multiple_of((heads[role] * 2 + 1 - side) * head_dim, head_dim)
            stage[role, :, lands] = w_ref[kind, :, pl.ds(start, head_dim)]
    pl.semaphore_wait(barrier, len(others))

    blocks = [
        (1 - pair) * 2 + pair,
        (1 - pair) * 2 + 1 - pair,
        mate,
    ]

    def cross(h):
        turn = jnp.where(near, 0, 1)
        return remote(
            tok_ref.at[pl.ds(h * short, short), held(1 - pair, t)], rows.at[c, h, t],
            cross_send.at[h], cross_recv.at[turn, h], at_clu(2 - pair),
        )

    def cross_came(n, h):
        here = rows.at[blocks[n], h, t]
        return remote(here, here, cross_send.at[h], cross_recv.at[n, h], at_clu(mate))

    def forward(n, h):
        here = rows.at[blocks[n], h, t]
        return remote(here, here, fwd_send.at[n, h], fwd_recv.at[n, h], at_clu(mate))

    def to_mate(h):
        return remote(
            tok_ref.at[pl.ds(h * short, short), held(pair, t)], rows.at[c, h, t],
            mate_send.at[h], mate_recv.at[h], at_clu(mate),
        )

    def mate_came(h):
        here = rows.at[mate, h, t]
        return remote(here, here, mate_send.at[h], mate_recv.at[h], at_clu(mate))

    def shared(n, h, q, send, recv, peer):
        here = rows.at[blocks[n], h, q]
        return remote(here, here, send.at[n, h], recv.at[n, h], peer)

    def to_core(n, h, q):
        return shared(n, h, q, core_send, core_recv, core_peer)

    def to_y(n, h, q):
        return shared(n, h, q, y_send, y_recv, y_peer)

    def to_core_far(n, h, q):
        return shared(n, h, q, far_send, far_recv, core_peer)

    def w_mate(role, e):
        return remote(
            stage.at[role, pl.ds(e * cut, cut)], piece(a, side, role, e),
            wm_send.at[role, e], wm_recv.at[role, e], at_clu(mate),
        )

    def w_mate_came(role, e):
        here = piece(a, 1 - side, role, e)
        return remote(here, here, wm_send.at[role, e], wm_recv.at[role, e], at_clu(mate))

    def w_cross(i, ctx, role, e):
        here = piece(ctx, side if i == 0 else 1 - side, role, e)
        return remote(here, here, wx_send.at[i, role, e], wx_recv.at[i, role, e], x_peer)

    def w_pass(role):
        for e in range(2):
            w_mate_came(role, e).wait_recv()
            w_cross(1, a, role, e).start()

    def w_ready(role):
        for i in range(2):
            for e in range(2):
                w_cross(i, 1 - a, role, e).wait_recv()

    def id_hop(d):
        goal = lax.rem(c + d, owners)
        return remote(marks.at[goal], ids.at[c], id_send.at[d - 1], id_recv.at[d - 1], at_clu(goal))

    def id_came(d):
        source = lax.rem(c + owners - d, owners)
        return remote(ids.at[source], ids.at[source], id_send.at[d - 1], id_recv.at[d - 1], at_clu(source))

    def part_hop(block, h):
        return remote(
            part.at[block, h], theirs.at[block, h],
            part_send.at[block, h], part_recv.at[block, h], at_clu(twin),
        )

    for h in range(2):
        cross(h).start()
    for role in range(2):
        for e in range(2):
            w_cross(0, a, role, e).start()
            if role == 0:
                w_mate(role, e).start()
        if role == 0:
            for h in range(2):
                to_mate(h).start()
    for d in range(1, owners):
        id_hop(d).start()

    def share(n, h):
        to_y(n, h, t).start()
        to_core(n, h, t).start()

    def relay(n):
        q = (1 - y) * 2 + k
        for h in range(2):
            to_y(n, h, q).wait_recv()
            to_core_far(n, h, q).start()

    def arrive_near(n):
        for h in range(2):
            cross_came(n, h).wait_recv()
            forward(n, h).start()
            share(n, h)

    def arrive_far(n):
        for h in range(2):
            forward(n, h).wait_recv()
            share(n, h)

    def whole(block, h):
        return jnp.concatenate([rows[block, h, q] for q in range(4)], axis=1)

    def give(block, h):
        given = jnp.dot(whole(block, h), weights[1 - pair], preferred_element_type=jnp.float32)
        part[block, h] = given.astype(jnp.bfloat16)
        part_hop(block, h).start()

    def finish(n):
        for h in range(2):
            to_core(n, h, y * 2 + 1 - k).wait_recv()
            to_core_far(n, h, (1 - y) * 2 + 1 - k).wait_recv()
            give(blocks[n], h)

    pl.when(near)(lambda: arrive_near(0))
    w_mate(1, 0).start()
    w_pass(0)
    pl.when(near)(lambda: arrive_near(1))
    w_mate(1, 1).start()
    for h in range(2):
        mate_came(h).wait_recv()
        share(2, h)
    pl.when(jnp.logical_not(near))(lambda: arrive_far(0))
    relay(2)
    for copy in local:
        copy.wait()
    w_ready(0)
    for h in range(2):
        give(c, h)
    finish(2)
    relay(0)
    finish(0)
    pl.when(jnp.logical_not(near))(lambda: arrive_far(1))
    w_pass(1)
    relay(1)
    finish(1)
    w_ready(1)
    for block in range(owners):
        both = jnp.concatenate([whole(block, h) for h in range(2)], axis=0)
        mine[block] = jnp.dot(both, weights[pair], preferred_element_type=jnp.float32)
    for d in range(1, owners):
        id_came(d).wait_recv()
    for block in range(owners):
        for h in range(2):
            part_hop(block, h).wait_recv()
            proj[block, h * short : (h + 1) * short] = (
                mine[block, h * short : (h + 1) * short] + theirs[block, h].astype(jnp.float32)
            ).astype(jnp.bfloat16)

    def send_reply(goal):
        return remote(
            reply.at[goal], out_ref.at[:, pl.ds(pl.multiple_of(c * head_dim, head_dim), head_dim)],
            out_send.at[goal], out_recv.at[c], at_clu(goal),
        )

    def keep_reply(goal):
        return pltpu.make_async_copy(
            reply.at[goal], out_ref.at[:, pl.ds(pl.multiple_of(c * head_dim, head_dim), head_dim)],
            out_send.at[goal],
        )

    for goal in reversed(range(owners)):
        query = proj[goal, :, :head_dim]
        query_ids = jnp.transpose(ids[goal])[:, :1]
        parts = []
        for block in range(goal + 1):
            scores = lax.dot_general(
                query, proj[block, :, :head_dim], (((1,), (1,)), ((), ())),
                preferred_element_type=jnp.float32,
            ) * (score_scale * LOG2E)
            admitted = query_ids == ids[block, :1, :]
            if block == goal:
                at = lax.broadcasted_iota(jnp.int32, (count, count), 0)
                to = lax.broadcasted_iota(jnp.int32, (count, count), 1)
                scores = jnp.where(at == to, -100000.0 * LOG2E, scores)
                admitted = admitted & (to <= at)
            parts.append(jnp.where(admitted, scores, -1e30))
        top = jnp.max(functools.reduce(jnp.maximum, parts), axis=1, keepdims=True)
        mixed = jnp.zeros((count, 2 * head_dim), jnp.float32)
        for block, piece_scores in enumerate(parts):
            weighed = jnp.exp2(piece_scores - top).astype(jnp.bfloat16)
            summands = jnp.concatenate(
                [proj[block, :, head_dim:], jnp.ones((count, head_dim), jnp.bfloat16)], axis=1
            )
            mixed += jnp.dot(weighed, summands, preferred_element_type=jnp.float32)
        reply[goal] = (mixed[:, :head_dim] / mixed[:, head_dim:]).astype(jnp.bfloat16)
        pl.when(c != goal)(lambda goal=goal: send_reply(goal).start())
        pl.when(c == goal)(lambda goal=goal: keep_reply(goal).start())

    for h in range(2):
        cross(h).wait_send()
        to_mate(h).wait_send()
        for n in range(2):
            pl.when(near)(lambda n=n, h=h: forward(n, h).wait_send())
        for n in range(3):
            to_y(n, h, t).wait_send()
            to_core(n, h, t).wait_send()
            to_core_far(n, h, (1 - y) * 2 + k).wait_send()
        for block in range(owners):
            part_hop(block, h).wait_send()
    for role in range(2):
        for e in range(2):
            w_mate(role, e).wait_send()
            for i in range(2):
                w_cross(i, a, role, e).wait_send()
    for d in range(1, owners):
        id_hop(d).wait_send()
    for goal in range(owners):
        @pl.when(c != goal)
        def _(goal=goal):
            send_reply(goal).wait_send()
            column = out_ref.at[:, pl.ds(goal * head_dim, head_dim)]
            remote(reply.at[goal], column, out_send.at[goal], out_recv.at[goal], at_clu(goal)).wait_recv()

        pl.when(c == goal)(lambda goal=goal: keep_reply(goal).wait())


def head_body(tokens, proj_weight, clusters):
    row_count, width = tokens.shape[1:]
    owners = lax.axis_size("clu")
    heads_here = clusters.shape[2]
    depth, _, proj_width = proj_weight.shape
    head_dim = proj_width // heads_here
    kinds = proj_weight.transpose(1, 0, 2)
    steps = owners - 1
    dma = pltpu.SemaphoreType.DMA
    split = (owners, 2, row_count // 2, 2 * head_dim)
    out = pl.pallas_call(
        functools.partial(head_kernel, owners, depth, head_dim, head_dim ** (-0.5)),
        out_shape=jax.ShapeDtypeStruct((row_count, proj_width), jnp.bfloat16),
        in_specs=[pl.BlockSpec(memory_space=space) for space in (pl.ANY, pltpu.VMEM, pltpu.VMEM)],
        out_specs=pl.BlockSpec(memory_space=pl.ANY),
        scratch_shapes=[
            pltpu.VMEM((owners, 2, 4, row_count // 2, width // 8), jnp.bfloat16),
            pltpu.VMEM((2, width // 2, 2 * head_dim), jnp.bfloat16),
            pltpu.VMEM((2, depth, 2 * head_dim), jnp.bfloat16),
            pltpu.VMEM((owners, 8, row_count), jnp.int32),
            pltpu.VMEM((owners, 8, row_count), jnp.int32),
            pltpu.VMEM((owners, row_count, 2 * head_dim), jnp.float32),
            pltpu.VMEM(split, jnp.bfloat16),
            pltpu.VMEM(split, jnp.bfloat16),
            pltpu.VMEM((owners, row_count, 2 * head_dim), jnp.bfloat16),
            pltpu.VMEM((owners, row_count, head_dim), jnp.bfloat16),
            dma((8,)),
            dma((2, 2)), dma((2, 2)),
            dma((2, 2, 2)), dma((2, 2, 2)),
            dma((steps,)), dma((steps,)),
            dma((2,)), dma((2, 2)),
            dma((2, 2)), dma((2, 2)),
            dma((2,)), dma((2,)),
            dma((3, 2)), dma((3, 2)),
            dma((3, 2)), dma((3, 2)),
            dma((3, 2)), dma((3, 2)),
            dma((owners, 2)), dma((owners, 2)),
            dma((owners,)), dma((owners,)),
        ],
        compiler_params=pltpu.CompilerParams(
            collective_id=0, has_side_effects=True, vmem_limit_bytes=40 * 1024 * 1024
        ),
    )(tokens[0], kinds, clusters[0].T)
    return out[None]


def body(tokens, proj_weight, clusters):
    local_rows = tokens[0]
    row_count = local_rows.shape[0]
    owners = lax.axis_size("clu")
    heads_here = clusters.shape[2]
    proj_width = proj_weight.shape[2]
    head_dim = proj_width // heads_here
    capacity = 2 * row_count // owners
    per_owner = CLUSTERS // owners
    length = row_count * owners
    total_slots = owners * capacity
    score_scale = head_dim ** (-0.5)
    weight_piece = lax.all_gather(proj_weight, ("ctx", "clu"), axis=0, tiled=True)
    flat_piece = weight_piece.reshape(weight_piece.shape[0], 2 * proj_width)
    summed = jnp.dot(local_rows, flat_piece, preferred_element_type=jnp.float32)
    projected = summed.astype(jnp.bfloat16)
    queries = projected[:, :proj_width].reshape(row_count, heads_here, head_dim)
    values = projected[:, proj_width:].reshape(row_count, heads_here, head_dim)
    features = jnp.concatenate([queries, values], axis=2).transpose(1, 0, 2)
    cluster_ids = clusters[0]
    owner_of = cluster_ids // per_owner
    onehot = (owner_of[:, :, None] == jnp.arange(owners, dtype=jnp.int32)[None, None, :]).astype(
        jnp.int32
    )
    rank_in = jnp.sum((jnp.cumsum(onehot, axis=0) - onehot) * onehot, axis=2)
    slot_of = (owner_of * capacity + rank_in).T
    head_rows = jnp.arange(heads_here, dtype=jnp.int32)[:, None]
    token_index = jnp.broadcast_to(
        jnp.arange(row_count, dtype=jnp.int32)[None, :], (heads_here, row_count)
    )
    source = jnp.zeros((heads_here, total_slots), jnp.int32).at[head_rows, slot_of].set(token_index)
    positions = lax.axis_index("clu") * row_count + jnp.arange(row_count, dtype=jnp.int32)
    labels = cluster_ids.T * length + positions[None, :]
    slot_tags = (
        jnp.full((heads_here, total_slots), -1, jnp.int32).at[head_rows, slot_of].set(labels)
    )
    outgoing = jnp.take_along_axis(features, source[:, :, None], axis=1)
    outgoing = jnp.where((slot_tags >= 0)[:, :, None], outgoing, jnp.zeros_like(outgoing))
    outgoing = outgoing.reshape(heads_here, owners, capacity, 2 * head_dim)
    slot_tags = slot_tags.reshape(heads_here, owners, capacity)

    def attend_head(head_item):
        slot_block, key_tags = head_item
        flattened = slot_block.reshape(-1, 2 * head_dim)
        key_rows = flattened[:, :head_dim]
        value_rows = flattened[:, head_dim:]
        key_tags = key_tags.reshape(-1)
        scores = (
            jnp.einsum("qd,kd->qk", key_rows, key_rows, preferred_element_type=jnp.float32)
            * score_scale
        )
        tag_group = key_tags // length
        tag_pos = key_tags % length
        admitted = (
            (key_tags[None, :] >= 0)
            & (tag_group[None, :] == tag_group[:, None])
            & (tag_pos[None, :] <= tag_pos[:, None])
        )
        scores = jnp.where(key_tags[None, :] == key_tags[:, None], -100000.0, scores)
        scores = jnp.where(admitted, scores, -1e30)
        row_max = jnp.max(scores, axis=1, keepdims=True)
        exp_scores = jnp.exp(scores - row_max)
        row_total = jnp.sum(exp_scores, axis=1, keepdims=True)
        probabilities = (exp_scores / row_total).astype(jnp.bfloat16)
        result = jnp.dot(probabilities, value_rows, preferred_element_type=jnp.float32).astype(
            jnp.bfloat16
        )
        return result.reshape(slot_block.shape[0], slot_block.shape[1], head_dim)

    replies = lax.map(
        attend_head,
        (
            lax.all_to_all(outgoing, "clu", split_axis=1, concat_axis=1, tiled=True),
            lax.all_to_all(slot_tags, "clu", split_axis=1, concat_axis=1, tiled=True),
        ),
    )
    returned = lax.all_to_all(replies, "clu", split_axis=1, concat_axis=1, tiled=True)
    returned = returned.reshape(heads_here, total_slots, head_dim)
    gathered = jnp.take_along_axis(returned, slot_of[:, :, None], axis=1)
    return gathered.transpose(1, 0, 2).reshape(1, row_count, heads_here * head_dim)


def solution(mesh):
    sizes = dict(mesh.shape)
    heads_here = 16 // sizes["tp"]
    by_head = sizes["ctx"] == 2 and sizes["tp"] == 4 and sizes["clu"] == heads_here == 4
    return jax.shard_map(
        head_body if by_head else body,
        mesh=mesh,
        in_specs=(P("ctx", "clu", None), P(("ctx", "clu"), None, "tp"), P("ctx", "clu", "tp")),
        out_specs=P("ctx", "clu", "tp"),
        check_vma=False,
    )
```
